128 devices in a mesh: row: 8 (over z, y_lo), col: 16 (over x, y_hi, core).
Axes of the slice: x: 4, y: 4 (y_hi: 2, y_lo: 2; y = y_hi * 2 + y_lo), z: 4, core: 2. Of those that a mesh axis runs over, the one named last changes fastest.
Arguments:
- surface: float32 [2048, 16384], P('row', 'col'), may hold values from -6 to 6
- potential: float32 [2048, 16384], P('row', 'col'), may hold values from -6 to 6
- depth_codes: int32 [2048, 16384], P('row', 'col'), may hold values from 0 to 7
- class_depth: float32 [8], replicated, may hold values from 0.5 to 2
- class_length: float32 [8], replicated, may hold values from 32 to 65536
- ship_rows: int32 [32], replicated, may hold values from 0 to 2047
- ship_cols: int32 [32], replicated, may hold values from 0 to 16383
- ship_reach: int32 [32], replicated, may hold values from 2 to 8
- ship_strength: float32 [32], replicated, may hold values from 0.5 to 2
Outputs:
- surface_next: float32 [2048, 16384], P('row', 'col')
- potential_next: float32 [2048, 16384], P('row', 'col')
The draws below stay inside these ranges and needn't reach their ends.
All inputs are finite; a program needn't handle non-finite values.
Results may differ from the reference program's by a relative error of at most 0.0003.
Values sent between devices are 32-bit elements; how exact they have to be, the bound alone decides.
A program may use at most 64 MiB of HBM per device.

```python
import math
import jax
import jax.numpy as jnp
from jax import lax

CY = 256
CX = 1024
CLASSES = 8
SHIPS = 32
NY = 2048
NX = 16384


def with_ends(array, stream_key, low, top_value):
    extent = array.shape
    place = [jax.random.randint(jax.random.fold_in(stream_key, axis), (), 0, extent[axis]) for axis in range(len(extent))]
    array = array.at[tuple(place)].set(low)
    longest = extent.index(max(extent))
    place[longest] = (place[longest] + 1) % extent[longest]
    return array.at[tuple(place)].set(top_value)


def steps_of(rng, shape, cuts, smallest, largest):
    factor_of, own = 1.0, jax.random.fold_in(rng, 6)
    for dim, blocks in cuts:
        draws = jnp.exp(jax.random.uniform(jax.random.fold_in(own, dim), (blocks,), jnp.float32, smallest / len(cuts), largest / len(cuts)))
        factor_of = factor_of * jnp.repeat(draws, shape[dim] // blocks).reshape([-1 if axis == dim else 1 for axis in range(len(shape))])
    return factor_of


def noise(stream_key, extent, spread, most, split=(), kind=jnp.bfloat16):
    values = jax.random.normal(stream_key, extent, jnp.float32) * spread
    if len(split) > 0:
        values = steps_of(stream_key, extent, split, -0.22, 0.18) * values
    return jnp.clip(values, min=-most, max=most).astype(kind)


def setup_inputs(seed: int = 0) -> dict:
    arg_keys = jax.random.split(jax.random.key(seed), 10)
    surface = noise(arg_keys[0], (NY, NX), 1.0, 6.0, ((0, 8), (1, 16)), jnp.float32)
    potential = noise(arg_keys[1], (NY, NX), 1.0, 6.0, ((0, 8), (1, 16)), jnp.float32)
    depth_codes = with_ends(jax.random.randint(arg_keys[2], (NY, NX), 0, CLASSES), jax.random.fold_in(arg_keys[2], 1), 0, CLASSES - 1).astype(jnp.int32)
    class_depth = jnp.clip(jnp.exp(jax.random.uniform(arg_keys[3], (CLASSES,), jnp.float32, math.log(0.5), math.log(2.0))), 0.5, 2.0)
    class_length = jnp.clip(jnp.exp(jax.random.uniform(arg_keys[4], (CLASSES,), jnp.float32, math.log(32.0), math.log(65536.0))), 32.0, 65536.0)
    ship_rows = with_ends(jax.random.randint(arg_keys[5], (SHIPS,), 0, NY), jax.random.fold_in(arg_keys[5], 1), 0, NY - 1).astype(jnp.int32)
    ship_cols = with_ends(jax.random.randint(arg_keys[6], (SHIPS,), 0, NX), jax.random.fold_in(arg_keys[6], 1), 0, NX - 1).astype(jnp.int32)
    ship_reach = with_ends(jax.random.randint(arg_keys[7], (SHIPS,), 2, 9), jax.random.fold_in(arg_keys[7], 1), 2, 8).astype(jnp.int32)
    ship_strength = jnp.clip(jax.random.uniform(arg_keys[8], (SHIPS,), jnp.float32, 0.5, 2.0), 0.5, 2.0)
    return {"surface": surface, "potential": potential, "depth_codes": depth_codes, "class_depth": class_depth, "class_length": class_length, "ship_rows": ship_rows, "ship_cols": ship_cols, "ship_reach": ship_reach, "ship_strength": ship_strength}


def combine(earlier, later):
    return (earlier[0] * later[0], later[1] + later[0] * earlier[1])


def lookup(codes, table):
    result = jnp.zeros(codes.shape, jnp.float32)
    for klass in range(table.shape[0]):
        result = jnp.where(codes == klass, table[klass], result)
    return result


def divergence(padded_field, padded_depth):
    height = padded_field.shape[0]
    width = padded_field.shape[1]
    centre = padded_field[1:-1, 1:-1]
    centre_depth = padded_depth[1:-1, 1:-1]
    total = jnp.zeros(centre.shape, jnp.float32)
    for shift_y, shift_x in ((1, 0), (-1, 0), (0, 1), (0, -1)):
        other = padded_field[1 + shift_y:height - 1 + shift_y, 1 + shift_x:width - 1 + shift_x]
        other_depth = padded_depth[1 + shift_y:height - 1 + shift_y, 1 + shift_x:width - 1 + shift_x]
        face = 2.0 * centre_depth * other_depth / (centre_depth + other_depth)
        total = total + face * (other - centre)
    return total


def ship_pressure(rows, cols, reach, strength, row_start, row_count, col_start, col_count):
    widths = (reach + 1).astype(jnp.float32)
    row_index = row_start + jnp.arange(row_count, dtype=jnp.int32)
    col_index = col_start + jnp.arange(col_count, dtype=jnp.int32)
    along_y = jnp.maximum(0.0, 1.0 - jnp.abs(row_index[None, :] - rows[:, None]).astype(jnp.float32) / widths[:, None])
    along_x = jnp.maximum(0.0, 1.0 - jnp.abs(col_index[None, :] - cols[:, None]).astype(jnp.float32) / widths[:, None])
    along_y = along_y * strength[:, None]
    return jnp.dot(along_y.T, along_x, precision=lax.Precision.HIGHEST, preferred_element_type=jnp.float32)


def doubling(factor, offset, axis, reverse):
    length = factor.shape[axis]
    step = 1
    while step < length:
        if reverse:
            tail_factor = lax.slice_in_dim(factor, step, length, axis=axis)
            tail_offset = lax.slice_in_dim(offset, step, length, axis=axis)
            ones_part = jnp.ones_like(lax.slice_in_dim(factor, 0, step, axis=axis))
            zero_part = jnp.zeros_like(lax.slice_in_dim(offset, 0, step, axis=axis))
            prior_factor = jnp.concatenate([tail_factor, ones_part], axis=axis)
            prior_offset = jnp.concatenate([tail_offset, zero_part], axis=axis)
        else:
            head_factor = lax.slice_in_dim(factor, 0, length - step, axis=axis)
            head_offset = lax.slice_in_dim(offset, 0, length - step, axis=axis)
            ones_part = jnp.ones_like(lax.slice_in_dim(factor, 0, step, axis=axis))
            zero_part = jnp.zeros_like(lax.slice_in_dim(offset, 0, step, axis=axis))
            prior_factor = jnp.concatenate([ones_part, head_factor], axis=axis)
            prior_offset = jnp.concatenate([zero_part, head_offset], axis=axis)
        offset = offset + factor * prior_offset
        factor = factor * prior_factor
        step = step * 2
    return factor, offset


def local_scan(values, rates, axis, reverse):
    length = values.shape[axis]
    block = math.gcd(length, 128)
    count = length // block
    shape = values.shape[:axis] + (count, block) + values.shape[axis + 1:]
    factor = rates.reshape(shape)
    offset = ((1.0 - rates) * values).reshape(shape)
    factor, offset = doubling(factor, offset, axis + 1, reverse)
    edge = 0 if reverse else block - 1
    total_factor = lax.index_in_dim(factor, edge, axis=axis + 1, keepdims=False)
    total_offset = lax.index_in_dim(offset, edge, axis=axis + 1, keepdims=False)
    total_factor, total_offset = doubling(total_factor, total_offset, axis, reverse)
    zero_part = jnp.zeros_like(lax.slice_in_dim(total_offset, 0, 1, axis=axis))
    ones_part = jnp.ones_like(zero_part)
    if reverse:
        carry_offset = jnp.concatenate([lax.slice_in_dim(total_offset, 1, count, axis=axis), zero_part], axis=axis)
        carry_factor = jnp.concatenate([lax.slice_in_dim(total_factor, 1, count, axis=axis), ones_part], axis=axis)
    else:
        carry_offset = jnp.concatenate([zero_part, lax.slice_in_dim(total_offset, 0, count - 1, axis=axis)], axis=axis)
        carry_factor = jnp.concatenate([ones_part, lax.slice_in_dim(total_factor, 0, count - 1, axis=axis)], axis=axis)
    carry_offset = jnp.expand_dims(carry_offset, axis + 1)
    carry_factor = jnp.expand_dims(carry_factor, axis + 1)
    result_offset = offset + factor * carry_offset
    result_factor = factor * carry_factor
    return result_factor.reshape(values.shape), result_offset.reshape(values.shape)


def both_sweeps(values, rates, axis):
    forward = local_scan(values, rates, axis, False)[1]
    return local_scan(forward, rates, axis, True)[1]


def line_solve(values, rates, block):
    count = values.shape[0]
    value_blocks = values.reshape(count // block, block, values.shape[1])
    rate_blocks = rates.reshape(count // block, block, values.shape[1])

    def solve_block(pair):
        return both_sweeps(pair[0], pair[1], 1)

    return lax.map(solve_block, (value_blocks, rate_blocks)).reshape(values.shape)


def reference(surface, potential, depth_codes, class_depth, class_length, ship_rows, ship_cols, ship_reach, ship_strength):
    depth = lookup(depth_codes, class_depth)
    rates = jnp.exp(-1.0 / lookup(depth_codes, class_length))
    flow = divergence(jnp.pad(potential, 1), jnp.pad(depth, 1))
    surface_next = surface + 0.2 * flow
    pressure = ship_pressure(ship_rows, ship_cols, ship_reach, ship_strength, 0, NY, 0, NX)
    source = potential - 0.2 * (surface_next + pressure)
    xsolved = line_solve(source, rates, CY)
    potential_next = line_solve(xsolved.T, rates.T, CX).T
    return surface_next, potential_next
```

```python
import functools

import jax
import jax.numpy as jnp
from jax import lax
from jax.experimental import pallas as pl
from jax.experimental.pallas import tpu as pltpu
from jax.sharding import PartitionSpec as P

MESH = pl.DeviceIdType.MESH
F32 = jnp.float32
ROWS, COLS = 256, 1024
RI, RS = 32, 8
CJ, CC = 128, 8
QN, QL = 4, 32
LANES = 128
SHIPS = 32


def sub_iota():
    return lax.broadcasted_iota(jnp.int32, (8, LANES), 0)


def wide_iota(width):
    return lax.broadcasted_iota(jnp.int32, (8, width), 0)


def from_before(x, k, fill):
    return jnp.where(wide_iota(x.shape[1]) >= k, pltpu.roll(x, k, 0), fill)


def from_after(x, k, fill):
    return jnp.where(wide_iota(x.shape[1]) < 8 - k, pltpu.roll(x, 8 - k, 0), fill)


def prefix_pair(a, b):
    for k in (1, 2, 4):
        b = a * from_before(b, k, 0.0) + b
        a = a * from_before(a, k, 1.0)
    return a, b


def suffix_pair(a, c):
    for k in (1, 2, 4):
        c = c + a * from_after(c, k, 0.0)
        a = a * from_after(a, k, 1.0)
    return a, c


def suffix_bounce(a, d):
    for k in (1, 2, 4):
        d = d + a * from_after(d, k, 0.0) * a
        a = a * from_after(a, k, 1.0)
    return a, d


def carry_factors(a, d):
    count = len(a)
    after_a, after_d = [None] * count, [None] * count
    run_a, run_d = jnp.ones_like(a[0]), jnp.zeros_like(a[0])
    for q in reversed(range(count)):
        after_a[q], after_d[q] = run_a, run_d
        run_d = d[q] + a[q] * run_d * a[q]
        run_a = a[q] * run_a
    before = jnp.ones_like(run_a)
    for k in (1,):
        inclusive, _ = prefix_pair(run_a, jnp.zeros_like(run_a))
        before = from_before(inclusive, k, 1.0)
    all_a, all_d = suffix_bounce(run_a, run_d)
    out_a, out_d = from_after(all_a, 1, 1.0), from_after(all_d, 1, 0.0)
    result = []
    for q in range(count):
        right_a = out_a * after_a[q]
        right_d = after_d[q] + after_a[q] * out_d * after_a[q]
        result.append((before, right_a, before * a[q] * right_d))
        before = before * a[q]
    return result, all_a, all_d


def carry_values(a, b, c, d):
    count = len(a)
    run_a, run_b = a[0], b[0]
    for q in range(1, count):
        run_b = a[q] * run_b + b[q]
        run_a = a[q] * run_a
    _, inclusive = prefix_pair(run_a, run_b)
    left = [from_before(inclusive, 1, 0.0)]
    for q in range(count - 1):
        left.append(a[q] * left[q] + b[q])
    c = [c[q] + d[q] * left[q] for q in range(count)]
    run_c = c[count - 1]
    for q in reversed(range(count - 1)):
        run_c = c[q] + a[q] * run_c
    _, inclusive = suffix_pair(run_a, run_c)
    right = [None] * count
    right[count - 1] = from_after(inclusive, 1, 0.0)
    for q in reversed(range(1, count)):
        right[q - 1] = a[q] * right[q] + c[q]
    return left, right


def kernel(
    nrow,
    ncol,
    depth_s, length_s, srow_s, scol_s, sreach_s, sstr_s,
    pot_h, code_h, surf_h,
    sn_h, out_h,
    cN, pN, sN, prN, uN, iaN, rN, GN, HN, bN, xN,
    GyC, HyC, Gy, Hy, WGy, WHy, fN,
    rT, iaT, wT, pT, uT, GcT, HcT, GT, HT, dT, sT, fT,
    fB, bB, hp, hc,
    eb, lb, ye, yl, xin,
    in_sem, out_sem, h_send, h_recv, e_send, e_recv, l_send, l_recv,
    ye_send, ye_recv, yl_send, yl_recv,
):
    r = lax.axis_index("row")
    c = lax.axis_index("col")

    def loads(src, dst, k):
        return [
            pltpu.make_async_copy(src.at[s], dst.at[:, s, :], in_sem.at[k, s]) for s in range(RS)
        ]

    code_in = loads(code_h, cN, 0)
    pot_in = loads(pot_h, pN, 1)
    surf_in = loads(surf_h, sN, 2)
    for cp in code_in + pot_in + surf_in:
        cp.start()

    barrier = pltpu.get_barrier_semaphore()
    north, south = lax.rem(r + nrow - 1, nrow), lax.rem(r + 1, nrow)
    for k in [1, nrow - 1] + list(range(2, nrow - 1)):
        pl.semaphore_signal(
            barrier, inc=1, device_id=(lax.rem(r + k, nrow), c), device_id_type=MESH
        )
    for k in range(1, ncol):
        pl.semaphore_signal(
            barrier, inc=1, device_id=(r, lax.rem(c + k, ncol)), device_id_type=MESH
        )

    sub = sub_iota()
    tab_len = jnp.zeros((8, LANES), F32)
    tab_dep = jnp.zeros((8, LANES), F32)
    for k in range(8):
        tab_len = jnp.where(sub == k, length_s[k], tab_len)
        tab_dep = jnp.where(sub == k, depth_s[k], tab_dep)
    tab_r = jnp.exp(-1.0 / tab_len)
    tab_w = (1.0 - tab_r) / tab_r
    tab_ia = 1.0 / tab_dep

    def look(tab, idx):
        return jnp.take_along_axis(tab, idx, axis=0)

    sub32 = lax.broadcasted_iota(jnp.int32, (SHIPS, LANES), 0)
    p_row = jnp.zeros((SHIPS, LANES), jnp.int32)
    p_col = jnp.zeros((SHIPS, LANES), jnp.int32)
    p_wid = jnp.ones((SHIPS, LANES), F32)
    p_str = jnp.zeros((SHIPS, LANES), F32)
    for k in range(SHIPS):
        p_row = jnp.where(sub32 == k, srow_s[k], p_row)
        p_col = jnp.where(sub32 == k, scol_s[k], p_col)
        p_wid = jnp.where(sub32 == k, (sreach_s[k] + 1).astype(F32), p_wid)
        p_str = jnp.where(sub32 == k, sstr_s[k], p_str)
    lane32 = lax.broadcasted_iota(jnp.int32, (SHIPS, LANES), 1)
    parts = []
    for g in range(2):
        held = lane32 + g * LANES
        y = r * ROWS + lax.bitwise_and(held, 7) * RI + lax.shift_right_logical(held, 3)
        near = jnp.maximum(0.0, 1.0 - jnp.abs(y - p_row).astype(F32) / p_wid)
        parts.append((near * p_str).T)
    along_y = jnp.concatenate(parts, axis=0)

    @pl.loop(0, CC)
    def _(cc):
        x = c * COLS + cc * LANES + lane32
        near = jnp.maximum(0.0, 1.0 - jnp.abs(x - p_col).astype(F32) / p_wid)
        block = jnp.dot(
            along_y, near, precision=lax.Precision.HIGHEST, preferred_element_type=F32
        )
        prN[:, :, pl.ds(pl.multiple_of(cc * LANES, LANES), LANES)] = block.reshape(RI, RS, LANES)

    for cp in code_in:
        cp.wait()

    def cols(cc):
        return pl.ds(pl.multiple_of(cc * LANES, LANES), LANES)

    def block_of(ref, g, cc):
        return ref[pl.ds(g * 16, 16), :, cols(cc)].reshape(LANES, LANES)

    def put_t(ref, g, cc, value):
        ref.at[g][pl.ds(cc, CJ, stride=CC), :] = value

    def get_t(ref, g, cc):
        return ref.at[g][pl.ds(cc, CJ, stride=CC), :]

    @pl.loop(0, CC)
    def _(cc):
        for g in range(2):
            idx = block_of(cN, g, cc).T.reshape(16, 8, LANES)
            for tab, ref in ((tab_r, rT), (tab_ia, iaT), (tab_w, wT)):
                put_t(
                    ref, g, cc,
                    jnp.concatenate([look(tab, idx[k]) for k in range(16)], axis=0),
                )

    def row8(j):
        return pl.ds(pl.multiple_of(j * 8, 8), 8)

    one = jnp.ones((8, LANES), F32)
    zero = jnp.zeros((8, LANES), F32)
    chains = [(q, g) for q in range(QN) for g in range(2)]

    def fwd(i, carry):
        new = []
        for n, (q, g) in enumerate(chains):
            f = carry[n] * rT[g, row8(q * QL + i), :]
            fT[g, row8(q * QL + i), :] = f
            new.append(f)
        return tuple(new)

    xa = lax.fori_loop(0, QL, fwd, (one,) * 8)

    def bwd(t, carry):
        i = QL - 1 - t
        new = []
        for n, (q, g) in enumerate(chains):
            at = row8(q * QL + i)
            rate = rT[g, at, :]
            grow = carry[2 * n] * rate
            bounce = (1.0 - rate) * fT[g, at, :] + rate * carry[2 * n + 1]
            GcT[g, at, :] = grow
            HcT[g, at, :] = bounce
            new += [grow, bounce]
        return tuple(new)

    ends = lax.fori_loop(0, QL, bwd, (one, zero) * 8)
    xd = ends[1::2]
    xA = [[xa[q * 2 + g] for q in range(QN)] for g in range(2)]
    xD = [[xd[q * 2 + g] for q in range(QN)] for g in range(2)]
    line_a, line_d = [], []
    for g in range(2):
        factors, all_a, all_d = carry_factors(xA[g], xD[g])
        line_a.append(all_a[0:1])
        line_d.append(all_d[0:1])
        for q in range(QN):
            left, right, turn = factors[q]

            def scale(i, _, g=g, q=q, left=left, right=right, turn=turn):
                at = row8(q * QL + i)
                grow = GcT[g, at, :]
                GT[g, at, :] = grow * right
                HT[g, at, :] = grow * turn + HcT[g, at, :] * left
                return 0

            lax.fori_loop(0, QL, scale, 0, unroll=4)

    for cp in pot_in:
        cp.wait()

    @pl.loop(0, CC)
    def _(cc):
        for g in range(2):
            put_t(pT, g, cc, block_of(pN, g, cc).T)

    last = CJ * CC - 1
    for g in range(2):
        eb[c, 0, pl.ds(g, 1), :] = line_a[g]
        eb[c, 1, pl.ds(g, 1), :] = line_d[g]
        eb[c, 2, pl.ds(g, 1), :] = pT[g, pl.ds(0, 1), :]
        eb[c, 3, pl.ds(g, 1), :] = pT[g, pl.ds(last, 1), :]
        eb[c, 4, pl.ds(g, 1), :] = iaT[g, pl.ds(0, 1), :]
        eb[c, 5, pl.ds(g, 1), :] = iaT[g, pl.ds(last, 1), :]
        eb[c, 6, pl.ds(g, 1), :] = rT[g, pl.ds(0, 1), :]
        eb[c, 7, pl.ds(g, 1), :] = rT[g, pl.ds(last, 1), :]

    pl.semaphore_wait(barrier, nrow - 1 + ncol - 1)
    halo = []
    for n, (src_i, src_s, dst_s, target) in enumerate(
        ((RI - 1, RS - 1, 0, south), (0, 0, RS - 1, north))
    ):
        for m, (src, dst) in enumerate(((pN, hp), (cN, hc))):
            halo.append(
                pltpu.make_async_remote_copy(
                    src_ref=src.at[src_i, pl.ds(src_s, 1), :],
                    dst_ref=dst.at[n, pl.ds(dst_s, 1), :],
                    send_sem=h_send.at[n, m],
                    recv_sem=h_recv.at[n, m],
                    device_id=(target, c),
                    device_id_type=MESH,
                )
            )
    for cp in halo:
        cp.start()

    def to_row(buf, send, recv, k):
        return pltpu.make_async_remote_copy(
            src_ref=buf.at[c],
            dst_ref=buf.at[c],
            send_sem=send.at[k],
            recv_sem=recv.at[k],
            device_id=(r, lax.rem(c + k, ncol)),
            device_id_type=MESH,
        )

    def to_col(buf, send, recv, k):
        return pltpu.make_async_remote_copy(
            src_ref=buf.at[r],
            dst_ref=buf.at[r],
            send_sem=send.at[k],
            recv_sem=recv.at[k],
            device_id=(lax.rem(r + k, nrow), c),
            device_id_type=MESH,
        )

    early = [to_row(eb, e_send, e_recv, k) for k in range(1, ncol)]
    for cp in early:
        cp.start()

    @pl.loop(0, CC)
    def _(cc):
        for g in range(2):
            for src, dst in ((GT, GN), (HT, HN)):
                dst[pl.ds(g * 16, 16), :, cols(cc)] = get_t(src, g, cc).T.reshape(16, 8, LANES)

    for cp in surf_in:
        cp.wait()

    groups = range(CC)
    col_of = [pl.ds(cc * LANES, LANES) for cc in groups]

    def codes_row(i, _):
        for cc in groups:
            iaN[i, :, col_of[cc]] = look(tab_ia, cN[i, :, col_of[cc]])
        return 0

    lax.fori_loop(0, RI, codes_row, 0)

    def flux(ia0, ia1, p0, p1):
        return (2.0 / (ia0 + ia1)) * (p1 - p0)

    before = []
    for cc in groups:
        t = flux(
            iaN[RI - 1, :, col_of[cc]], pltpu.roll(iaN[0, :, col_of[cc]], 7, 0),
            pN[RI - 1, :, col_of[cc]], pltpu.roll(pN[0, :, col_of[cc]], 7, 0),
        )
        before.append(jnp.where(sub < 7, t, 0.0))
    closing = before
    before = tuple(pltpu.roll(t, 1, 0) for t in before)

    def flow_row(i, carry):
        new = []
        for cc in groups:
            t = flux(
                iaN[i, :, col_of[cc]], iaN[i + 1, :, col_of[cc]],
                pN[i, :, col_of[cc]], pN[i + 1, :, col_of[cc]],
            )
            uN[i, :, col_of[cc]] = sN[i, :, col_of[cc]] + 0.2 * (t - carry[cc])
            new.append(t)
        return tuple(new)

    before = lax.fori_loop(0, RI - 1, flow_row, before)
    for cc in groups:
        uN[RI - 1, :, col_of[cc]] = sN[RI - 1, :, col_of[cc]] + 0.2 * (closing[cc] - before[cc])

    def level_t():
        @pl.loop(0, CC)
        def _(cc):
            for g in range(2):
                put_t(uT, g, cc, (block_of(uN, g, cc) + block_of(prN, g, cc)).T)

    level_t()

    start = []
    for g in range(2):
        t = flux(
            iaT[g, row8(CJ - 1), :], pltpu.roll(iaT[g, row8(0), :], 7, 0),
            pT[g, row8(CJ - 1), :], pltpu.roll(pT[g, row8(0), :], 7, 0),
        )
        start.append(jnp.where(sub < 7, t, 0.0))

    def source_row(j, g, t, before, sum_b, sum_c):
        at = row8(j)
        d = t - before
        dT[g, at, :] = d
        value = pT[g, at, :] - 0.2 * (uT[g, at, :] + 0.2 * d)
        value = value * wT[g, at, :]
        return sum_b + value * GT[g, at, :], sum_c + value * HT[g, at, :]

    def source_loop(j, carry):
        new = []
        for g in range(2):
            before, sum_b, sum_c = carry[3 * g : 3 * g + 3]
            at, nxt = row8(j), row8(j + 1)
            t = flux(iaT[g, at, :], iaT[g, nxt, :], pT[g, at, :], pT[g, nxt, :])
            sum_b, sum_c = source_row(j, g, t, before, sum_b, sum_c)
            new += [t, sum_b, sum_c]
        return tuple(new)

    init = []
    for g in range(2):
        init += [pltpu.roll(start[g], 1, 0), zero, zero]
    sums = lax.fori_loop(0, CJ - 1, source_loop, tuple(init))
    line_b, line_c = [], []
    for g in range(2):
        sum_b, sum_c = source_row(CJ - 1, g, start[g], *sums[3 * g : 3 * g + 3])
        line_b.append(jnp.sum(sum_b, axis=0, keepdims=True))
        line_c.append(jnp.sum(sum_c, axis=0, keepdims=True))

    for cp in halo:
        cp.wait_recv()
    lane = lax.broadcasted_iota(jnp.int32, (1, LANES), 1)
    for n, (i, s, has) in enumerate(((0, 0, r > 0), (RI - 1, RS - 1, r < nrow - 1))):
        tot_b, tot_c = zero, zero
        here = jnp.logical_and(sub == s, has)
        for cc in groups:
            at = col_of[cc]
            code = cN[i, :, at]
            other = look(tab_ia, jnp.where(sub == s, hc[n, :, at], 0))
            q = flux(look(tab_ia, code), other, pN[i, :, at], hp[n, :, at])
            q = jnp.where(here, q, 0.0)
            uN[i, :, at] = uN[i, :, at] + 0.2 * q
            q = -0.04 * q * look(tab_w, code)
            tot_b = tot_b + q * GN[i, :, at]
            tot_c = tot_c + q * HN[i, :, at]
        mine = lane == (0 if n == 0 else LANES - 1)
        line_b[n] = line_b[n] + jnp.where(mine, jnp.sum(tot_b), 0.0)
        line_c[n] = line_c[n] + jnp.where(mine, jnp.sum(tot_c), 0.0)
    for g in range(2):
        lb[c, 0, pl.ds(g, 1), :] = line_b[g]
        lb[c, 1, pl.ds(g, 1), :] = line_c[g]
    late = [to_row(lb, l_send, l_recv, k) for k in range(1, ncol)]
    for cp in late:
        cp.start()

    def rates_row(i, carry):
        new = []
        for cc in groups:
            rate = look(tab_r, cN[i, :, col_of[cc]])
            rN[i, :, col_of[cc]] = rate
            f = carry[cc] * rate
            fN[i, :, col_of[cc]] = f
            new.append(f)
        return tuple(new)

    ya = lax.fori_loop(0, RI, rates_row, (one,) * 8)

    def bounce_row(t, carry):
        i = RI - 1 - t
        new = []
        for cc in groups:
            rate = rN[i, :, col_of[cc]]
            grow = carry[2 * cc] * rate
            bounce = (1.0 - rate) * fN[i, :, col_of[cc]] + rate * carry[2 * cc + 1]
            GyC[i, :, col_of[cc]] = grow
            HyC[i, :, col_of[cc]] = bounce
            new += [grow, bounce]
        return tuple(new)

    yd = lax.fori_loop(0, RI, bounce_row, (one, zero) * 8)[1::2]
    for cc in groups:
        factors, all_a, all_d = carry_factors([ya[cc]], [yd[cc]])
        left, right, turn = factors[0]
        ye[r, 0, pl.ds(cc, 1), :] = all_a[0:1]
        ye[r, 1, pl.ds(cc, 1), :] = all_d[0:1]

        def scale_row(i, _, cc=cc, left=left, right=right, turn=turn):
            at = col_of[cc]
            grow = GyC[i, :, at]
            full = grow * right
            turned = grow * turn + HyC[i, :, at] * left
            weight = look(tab_w, cN[i, :, at])
            Gy[i, :, at] = full
            Hy[i, :, at] = turned
            WGy[i, :, at] = full * weight
            WHy[i, :, at] = turned * weight
            return 0

        lax.fori_loop(0, RI, scale_row, 0, unroll=4)
    y_early = [to_col(ye, ye_send, ye_recv, k) for k in range(1, nrow)]
    for cp in y_early:
        cp.start()

    level_t()

    def x_fwd(i, carry):
        new = []
        for n, (q, g) in enumerate(chains):
            at = row8(q * QL + i)
            rate = rT[g, at, :]
            value = pT[g, at, :] - 0.2 * (uT[g, at, :] + 0.2 * dT[g, at, :])
            f = (1.0 - rate) * value + rate * carry[n]
            fT[g, at, :] = f
            new.append(f)
        return tuple(new)

    xb = lax.fori_loop(0, QL, x_fwd, (zero,) * 8)

    def x_bwd(t, carry):
        i = QL - 1 - t
        new = []
        for n, (q, g) in enumerate(chains):
            at = row8(q * QL + i)
            rate = rT[g, at, :]
            b = (1.0 - rate) * fT[g, at, :] + rate * carry[n]
            sT[g, at, :] = b
            new.append(b)
        return tuple(new)

    xc = lax.fori_loop(0, QL, x_bwd, (zero,) * 8)
    for g in range(2):
        left, right = carry_values(
            xA[g], [xb[q * 2 + g] for q in range(QN)], [xc[q * 2 + g] for q in range(QN)], xD[g]
        )
        for q in range(QN):

            def fix(i, _, g=g, q=q, fl=left[q], br=right[q]):
                at = row8(q * QL + i)
                sT[g, at, :] = sT[g, at, :] + GcT[g, at, :] * br + HcT[g, at, :] * fl
                return 0

            lax.fori_loop(0, QL, fix, 0, unroll=4)

    @pl.loop(0, CC)
    def _(cc):
        for g in range(2):
            bN[pl.ds(g * 16, 16), :, cols(cc)] = get_t(sT, g, cc).T.reshape(16, 8, LANES)

    for cp in early:
        cp.wait_recv()
    nil = jnp.zeros((2, LANES), F32)
    faces = []
    for j in range(ncol - 1):
        faces.append(
            0.04 * flux(eb[j, 5], eb[j + 1, 4], eb[j, 3], eb[j + 1, 2])
        )
    for j in range(ncol):
        r_w, r_e = eb[j, 6], eb[j, 7]
        west = faces[j - 1] if j > 0 else nil
        east = faces[j] if j < ncol - 1 else nil
        out_e = -(1.0 - r_e) * east
        xin[j, 0] = (1.0 - r_w) / r_w * west
        xin[j, 1] = out_e
        xin[j, 2] = (1.0 - r_e) / r_e * out_e
    for cp in late:
        cp.wait_recv()
    f = nil
    for j in range(ncol):
        f = f + xin[j, 0]
        xin[j, 0] = f
        f = eb[j, 0] * f + (lb[j, 0] + xin[j, 1])
    b = nil
    for j in reversed(range(ncol)):
        b = b + xin[j, 2]
        xin[j, 2] = b
        b = eb[j, 0] * b + (lb[j, 1] + eb[j, 1] * xin[j, 0])
    for g in range(2):
        for src, dst in ((0, fB), (2, bB)):
            line = xin[c, src, pl.ds(g, 1), :]
            dst[pl.ds(g * 16, 16), :, :] = (
                jnp.broadcast_to(line, (LANES, LANES)).T.reshape(16, 8, LANES)
            )

    def solved_row(i, carry):
        new = []
        fb, bb = fB[i], bB[i]
        for cc in groups:
            at = col_of[cc]
            value = bN[i, :, at] + GN[i, :, at] * bb + HN[i, :, at] * fb
            xN[i, :, at] = value
            new += [
                carry[2 * cc] + value * WGy[i, :, at],
                carry[2 * cc + 1] + value * WHy[i, :, at],
            ]
        return tuple(new)

    sums = lax.fori_loop(0, RI, solved_row, (zero,) * 16)
    for cc in groups:
        yl[r, 0, pl.ds(cc, 1), :] = jnp.sum(sums[2 * cc], axis=0, keepdims=True)
        yl[r, 1, pl.ds(cc, 1), :] = jnp.sum(sums[2 * cc + 1], axis=0, keepdims=True)
    y_late = [to_col(yl, yl_send, yl_recv, k) for k in range(1, nrow)]
    for cp in y_late:
        cp.start()

    def y_fwd(i, carry):
        new = []
        for cc in groups:
            at = col_of[cc]
            rate = rN[i, :, at]
            f = (1.0 - rate) * xN[i, :, at] + rate * carry[cc]
            fN[i, :, at] = f
            new.append(f)
        return tuple(new)

    yb = lax.fori_loop(0, RI, y_fwd, (zero,) * 8)

    def y_bwd(t, carry):
        i = RI - 1 - t
        new = []
        for cc in groups:
            at = col_of[cc]
            rate = rN[i, :, at]
            b = (1.0 - rate) * fN[i, :, at] + rate * carry[cc]
            xN[i, :, at] = b
            new.append(b)
        return tuple(new)

    yc = lax.fori_loop(0, RI, y_bwd, (zero,) * 8)
    for cc in groups:
        left, right = carry_values([ya[cc]], [yb[cc]], [yc[cc]], [yd[cc]])

        def fix_row(i, _, cc=cc, fl=left[0], br=right[0]):
            at = col_of[cc]
            xN[i, :, at] = xN[i, :, at] + GyC[i, :, at] * br + HyC[i, :, at] * fl
            return 0

        lax.fori_loop(0, RI, fix_row, 0, unroll=4)

    edge_w = jnp.where(c > 0, 1.0, 0.0)
    edge_e = jnp.where(c < ncol - 1, 1.0, 0.0)
    low, high = lax.rem(c + ncol - 1, ncol), lax.rem(c + 1, ncol)
    q_w = flux(eb[c, 4], eb[low, 5], eb[c, 2], eb[low, 3]) * edge_w
    q_e = flux(eb[c, 5], eb[high, 4], eb[c, 3], eb[high, 2]) * edge_e
    for g in range(2):
        dT[g, pl.ds(0, 1), :] = dT[g, pl.ds(0, 1), :] + q_w[g : g + 1]
        dT[g, pl.ds(last, 1), :] = dT[g, pl.ds(last, 1), :] + q_e[g : g + 1]

    @pl.loop(0, CC)
    def _(cc):
        for g in range(2):
            at = (pl.ds(g * 16, 16), slice(None), cols(cc))
            sN[at] = uN[at] + 0.2 * get_t(dT, g, cc).T.reshape(16, 8, LANES)

    sn_out = [
        pltpu.make_async_copy(sN.at[:, s, :], sn_h.at[s], out_sem.at[0, s]) for s in range(RS)
    ]
    for cp in sn_out:
        cp.start()

    for cp in y_early:
        cp.wait_recv()
    for cp in y_late:
        cp.wait_recv()
    f = zero
    fs = []
    for j in range(nrow):
        fs.append(f)
        f = ye[j, 0] * f + yl[j, 0]
    b = zero
    own_f, own_b = zero, zero
    for j in reversed(range(nrow)):
        own_f = jnp.where(r == j, fs[j], own_f)
        own_b = jnp.where(r == j, b, own_b)
        b = ye[j, 0] * b + (yl[j, 1] + ye[j, 1] * fs[j])
    rows_f = [jnp.broadcast_to(own_f[cc : cc + 1], (8, LANES)) for cc in groups]
    rows_b = [jnp.broadcast_to(own_b[cc : cc + 1], (8, LANES)) for cc in groups]

    def last_row(i, _):
        for cc in groups:
            at = col_of[cc]
            fN[i, :, at] = xN[i, :, at] + Gy[i, :, at] * rows_b[cc] + Hy[i, :, at] * rows_f[cc]
        return 0

    lax.fori_loop(0, RI, last_row, 0)
    pot_out = [
        pltpu.make_async_copy(fN.at[:, s, :], out_h.at[s], out_sem.at[1, s]) for s in range(RS)
    ]
    for cp in pot_out:
        cp.start()
    for cp in halo + early + late + y_early + y_late:
        cp.wait_send()
    for cp in sn_out + pot_out:
        cp.wait()


def shards(nrow, ncol, surface, potential, depth_codes, class_depth, class_length, ship_rows,
           ship_cols, ship_reach, ship_strength):
    tile = (RS, RI, COLS)
    natural = pltpu.VMEM((RI, RS, COLS), F32)
    turned = pltpu.VMEM((2, CJ * CC, LANES), F32)
    dma = pltpu.SemaphoreType.DMA
    smem = pl.BlockSpec(memory_space=pltpu.SMEM)
    hbm = pl.BlockSpec(memory_space=pl.ANY)
    surface_next, potential_next = pl.pallas_call(
        functools.partial(kernel, nrow, ncol),
        out_shape=[jax.ShapeDtypeStruct(tile, F32)] * 2,
        in_specs=[smem] * 6 + [hbm] * 3,
        out_specs=[hbm] * 2,
        scratch_shapes=[pltpu.VMEM((RI, RS, COLS), jnp.int32)]
        + [natural] * 17
        + [turned] * 12
        + [
            pltpu.VMEM((RI, RS, LANES), F32),
            pltpu.VMEM((RI, RS, LANES), F32),
            pltpu.VMEM((2, 8, COLS), F32),
            pltpu.VMEM((2, 8, COLS), jnp.int32),
            pltpu.VMEM((ncol, 8, 2, LANES), F32),
            pltpu.VMEM((ncol, 2, 2, LANES), F32),
            pltpu.VMEM((nrow, 2, 8, LANES), F32),
            pltpu.VMEM((nrow, 2, 8, LANES), F32),
            pltpu.VMEM((ncol, 3, 2, LANES), F32),
            dma((3, RS)), dma((2, RS)), dma((2, 2)), dma((2, 2)),
            dma((ncol,)), dma((ncol,)), dma((ncol,)), dma((ncol,)),
            dma((nrow,)), dma((nrow,)), dma((nrow,)), dma((nrow,)),
        ],
        compiler_params=pltpu.CompilerParams(
            collective_id=0, has_side_effects=True, vmem_limit_bytes=56 * 1024 * 1024
        ),
    )(
        class_depth, class_length, ship_rows, ship_cols, ship_reach, ship_strength,
        potential.reshape(tile), depth_codes.reshape(tile), surface.reshape(tile),
    )
    return surface_next.reshape(ROWS, COLS), potential_next.reshape(ROWS, COLS)


def solution(mesh):
    in_specs = (P("row", "col"), P("row", "col"), P("row", "col"), P(), P(), P(), P(), P(), P())
    out_specs = (P("row", "col"), P("row", "col"))
    return jax.shard_map(
        functools.partial(shards, mesh.shape["row"], mesh.shape["col"]),
        mesh=mesh, in_specs=in_specs, out_specs=out_specs, check_vma=False,
    )
```

```python
import functools

import jax
import jax.numpy as jnp
from jax import lax
from jax.experimental import pallas as pl
from jax.experimental.pallas import tpu as pltpu
from jax.sharding import PartitionSpec as P

MESH = pl.DeviceIdType.MESH
F32 = jnp.float32
ROWS, COLS = 256, 1024
RI, RS = 32, 8
CJ, CC = 128, 8
QN, QL = 4, 32
LANES = 128
SHIPS = 32


def sub_iota():
    return lax.broadcasted_iota(jnp.int32, (8, LANES), 0)


def wide_iota(width):
    return lax.broadcasted_iota(jnp.int32, (8, width), 0)


def from_before(x, k, fill):
    return jnp.where(wide_iota(x.shape[1]) >= k, pltpu.roll(x, k, 0), fill)


def from_after(x, k, fill):
    return jnp.where(wide_iota(x.shape[1]) < 8 - k, pltpu.roll(x, 8 - k, 0), fill)


def prefix_pair(a, b):
    for k in (1, 2, 4):
        b = a * from_before(b, k, 0.0) + b
        a = a * from_before(a, k, 1.0)
    return a, b


def suffix_pair(a, c):
    for k in (1, 2, 4):
        c = c + a * from_after(c, k, 0.0)
        a = a * from_after(a, k, 1.0)
    return a, c


def suffix_bounce(a, d):
    for k in (1, 2, 4):
        d = d + a * from_after(d, k, 0.0) * a
        a = a * from_after(a, k, 1.0)
    return a, d


def carry_factors(a, d):
    count = len(a)
    after_a, after_d = [None] * count, [None] * count
    run_a, run_d = jnp.ones_like(a[0]), jnp.zeros_like(a[0])
    for q in reversed(range(count)):
        after_a[q], after_d[q] = run_a, run_d
        run_d = d[q] + a[q] * run_d * a[q]
        run_a = a[q] * run_a
    before = jnp.ones_like(run_a)
    for k in (1,):
        inclusive, _ = prefix_pair(run_a, jnp.zeros_like(run_a))
        before = from_before(inclusive, k, 1.0)
    all_a, all_d = suffix_bounce(run_a, run_d)
    out_a, out_d = from_after(all_a, 1, 1.0), from_after(all_d, 1, 0.0)
    result = []
    for q in range(count):
        right_a = out_a * after_a[q]
        right_d = after_d[q] + after_a[q] * out_d * after_a[q]
        result.append((before, right_a, before * a[q] * right_d))
        before = before * a[q]
    return result, all_a, all_d


def carry_values(a, b, c, d):
    count = len(a)
    run_a, run_b = a[0], b[0]
    for q in range(1, count):
        run_b = a[q] * run_b + b[q]
        run_a = a[q] * run_a
    _, inclusive = prefix_pair(run_a, run_b)
    left = [from_before(inclusive, 1, 0.0)]
    for q in range(count - 1):
        left.append(a[q] * left[q] + b[q])
    c = [c[q] + d[q] * left[q] for q in range(count)]
    run_c = c[count - 1]
    for q in reversed(range(count - 1)):
        run_c = c[q] + a[q] * run_c
    _, inclusive = suffix_pair(run_a, run_c)
    right = [None] * count
    right[count - 1] = from_after(inclusive, 1, 0.0)
    for q in reversed(range(1, count)):
        right[q - 1] = a[q] * right[q] + c[q]
    return left, right


def kernel(
    nrow,
    ncol,
    depth_h, length_h, srow_h, scol_h, sreach_h, sstr_h,
    pot_h, code_h, surf_h,
    snN, xN, rN, GyC, HyC, inflow,
    cN, pN, sN, prN, uN, GN, HN, bN, fN,
    rT, iaT, pT, uT, GcT, HcT, dT, sT, fT,
    fB, bB, hp, hc,
    eb, lb, ye, yl, xin, xsc, ysc, yad, yfx,
    depth_s, length_s, srow_s, scol_s, sreach_s, sstr_s, s_sem,
    in_sem, h_send, h_recv, e_send, e_recv, l_send, l_recv,
    ye_send, ye_recv, yl_send, yl_recv,
):
    r = lax.axis_index("row")
    c = lax.axis_index("col")

    def loads(src, dst, k):
        return [
            pltpu.make_async_copy(src.at[s], dst.at[:, s, :], in_sem.at[k, s]) for s in range(RS)
        ]

    code_in = loads(code_h, cN, 0)
    pot_in = loads(pot_h, pN, 1)
    surf_in = loads(surf_h, sN, 2)
    small = [
        pltpu.make_async_copy(src, dst, s_sem.at[k])
        for k, (src, dst) in enumerate(
            (
                (depth_h, depth_s), (length_h, length_s), (srow_h, srow_s),
                (scol_h, scol_s), (sreach_h, sreach_s), (sstr_h, sstr_s),
            )
        )
    ]
    for cp in small + code_in + pot_in + surf_in:
        cp.start()

    barrier = pltpu.get_barrier_semaphore()
    north, south = lax.rem(r + nrow - 1, nrow), lax.rem(r + 1, nrow)
    for k in [1, nrow - 1] + list(range(2, nrow - 1)):
        pl.semaphore_signal(
            barrier, inc=1, device_id=(lax.rem(r + k, nrow), c), device_id_type=MESH
        )
    for k in range(1, ncol):
        pl.semaphore_signal(
            barrier, inc=1, device_id=(r, lax.rem(c + k, ncol)), device_id_type=MESH
        )

    for cp in small:
        cp.wait()
    sub = sub_iota()
    tab_len = jnp.zeros((8, LANES), F32)
    tab_dep = jnp.zeros((8, LANES), F32)
    for k in range(8):
        tab_len = jnp.where(sub == k, length_s[k], tab_len)
        tab_dep = jnp.where(sub == k, depth_s[k], tab_dep)
    tab_r = jnp.exp(-1.0 / tab_len)
    tab_w = (1.0 - tab_r) / tab_r
    tab_ia = 1.0 / tab_dep

    def look(tab, idx):
        return jnp.take_along_axis(tab, idx, axis=0)

    sub32 = lax.broadcasted_iota(jnp.int32, (SHIPS, LANES), 0)
    p_row = jnp.zeros((SHIPS, LANES), jnp.int32)
    p_col = jnp.zeros((SHIPS, LANES), jnp.int32)
    p_wid = jnp.ones((SHIPS, LANES), F32)
    p_str = jnp.zeros((SHIPS, LANES), F32)
    for k in range(SHIPS):
        p_row = jnp.where(sub32 == k, srow_s[k], p_row)
        p_col = jnp.where(sub32 == k, scol_s[k], p_col)
        p_wid = jnp.where(sub32 == k, (sreach_s[k] + 1).astype(F32), p_wid)
        p_str = jnp.where(sub32 == k, sstr_s[k], p_str)
    lane32 = lax.broadcasted_iota(jnp.int32, (SHIPS, LANES), 1)
    parts = []
    for g in range(2):
        held = lane32 + g * LANES
        y = r * ROWS + lax.bitwise_and(held, 7) * RI + lax.shift_right_logical(held, 3)
        near = jnp.maximum(0.0, 1.0 - jnp.abs(y - p_row).astype(F32) / p_wid)
        parts.append((near * p_str).T)
    along_y = jnp.concatenate(parts, axis=0)

    @pl.loop(0, CC)
    def _(cc):
        x = c * COLS + cc * LANES + lane32
        near = jnp.maximum(0.0, 1.0 - jnp.abs(x - p_col).astype(F32) / p_wid)
        block = jnp.dot(
            along_y, near, precision=lax.Precision.HIGHEST, preferred_element_type=F32
        )
        prN[:, :, pl.ds(pl.multiple_of(cc * LANES, LANES), LANES)] = block.reshape(RI, RS, LANES)

    for cp in code_in:
        cp.wait()

    def cols(cc):
        return pl.ds(pl.multiple_of(cc * LANES, LANES), LANES)

    def block_of(ref, g, cc):
        return ref[pl.ds(g * 16, 16), :, cols(cc)].reshape(LANES, LANES)

    def put_t(ref, g, cc, value):
        ref.at[g][pl.ds(cc, CJ, stride=CC), :] = value

    def get_t(ref, g, cc):
        return ref.at[g][pl.ds(cc, CJ, stride=CC), :]

    def blocks(body):
        @pl.loop(0, CC, unroll=2)
        def _(cc):
            for g in range(2):
                body(g, cc)

    def codes_block(g, cc):
        idx = block_of(cN, g, cc).T.reshape(16, 8, LANES)
        for tab, ref in ((tab_r, rT), (tab_ia, iaT)):
            put_t(ref, g, cc, jnp.concatenate([look(tab, idx[k]) for k in range(16)], axis=0))

    blocks(codes_block)

    def row8(j):
        return pl.ds(pl.multiple_of(j * 8, 8), 8)

    one = jnp.ones((8, LANES), F32)
    zero = jnp.zeros((8, LANES), F32)
    chains = [(q, g) for q in range(QN) for g in range(2)]

    def fwd(i, carry):
        new = []
        for n, (q, g) in enumerate(chains):
            at = row8(q * QL + i)
            fT[g, at, :] = carry[n]
            new.append(carry[n] * rT[g, at, :])
        return tuple(new)

    xa = lax.fori_loop(0, QL, fwd, (one,) * 8, unroll=4)

    def bwd(t, carry):
        i = QL - 1 - t
        new = []
        for n, (q, g) in enumerate(chains):
            at = row8(q * QL + i)
            rate = rT[g, at, :]
            grow = carry[2 * n]
            bounce = (1.0 - rate) * fT[g, at, :] + carry[2 * n + 1]
            GcT[g, at, :] = grow
            HcT[g, at, :] = bounce
            new += [rate * grow, rate * bounce]
        return tuple(new)

    ends = lax.fori_loop(0, QL, bwd, (one, zero) * 8, unroll=2)
    xd = ends[1::2]
    xA = [[xa[q * 2 + g] for q in range(QN)] for g in range(2)]
    xD = [[xd[q * 2 + g] for q in range(QN)] for g in range(2)]
    line_a, line_d, x_factors = [], [], []
    for g in range(2):
        factors, all_a, all_d = carry_factors(xA[g], xD[g])
        line_a.append(all_a[0:1])
        line_d.append(all_d[0:1])
        x_factors.append(factors)
        for q in range(QN):
            for k in range(3):
                xsc[g, q, k] = factors[q][k]

    for cp in pot_in:
        cp.wait()

    blocks(lambda g, cc: put_t(pT, g, cc, block_of(pN, g, cc).T))

    last = CJ * CC - 1
    for g in range(2):
        eb[c, 0, pl.ds(g, 1), :] = line_a[g]
        eb[c, 1, pl.ds(g, 1), :] = line_d[g]
        eb[c, 2, pl.ds(g, 1), :] = pT[g, pl.ds(0, 1), :]
        eb[c, 3, pl.ds(g, 1), :] = pT[g, pl.ds(last, 1), :]
        eb[c, 4, pl.ds(g, 1), :] = iaT[g, pl.ds(0, 1), :]
        eb[c, 5, pl.ds(g, 1), :] = iaT[g, pl.ds(last, 1), :]
        eb[c, 6, pl.ds(g, 1), :] = rT[g, pl.ds(0, 1), :]
        eb[c, 7, pl.ds(g, 1), :] = rT[g, pl.ds(last, 1), :]

    pl.semaphore_wait(barrier, nrow - 1 + ncol - 1)
    halo = []
    for n, (src_i, src_s, dst_s, target) in enumerate(
        ((RI - 1, RS - 1, 0, south), (0, 0, RS - 1, north))
    ):
        for m, (src, dst) in enumerate(((pN, hp), (cN, hc))):
            halo.append(
                pltpu.make_async_remote_copy(
                    src_ref=src.at[src_i, pl.ds(src_s, 1), :],
                    dst_ref=dst.at[n, pl.ds(dst_s, 1), :],
                    send_sem=h_send.at[n, m],
                    recv_sem=h_recv.at[n, m],
                    device_id=(target, c),
                    device_id_type=MESH,
                )
            )
    for cp in halo:
        cp.start()

    def to_row(buf, send, recv, k):
        return pltpu.make_async_remote_copy(
            src_ref=buf.at[c],
            dst_ref=buf.at[c],
            send_sem=send.at[k],
            recv_sem=recv.at[k],
            device_id=(r, lax.rem(c + k, ncol)),
            device_id_type=MESH,
        )

    def to_col(buf, send, recv, k):
        return pltpu.make_async_remote_copy(
            src_ref=buf.at[r],
            dst_ref=buf.at[r],
            send_sem=send.at[k],
            recv_sem=recv.at[k],
            device_id=(lax.rem(r + k, nrow), c),
            device_id_type=MESH,
        )

    early = [to_row(eb, e_send, e_recv, k) for k in range(1, ncol)]
    for cp in early:
        cp.start()

    for cp in surf_in:
        cp.wait()

    groups = range(CC)
    col_of = [pl.ds(cc * LANES, LANES) for cc in groups]

    def flux(ia0, ia1, p0, p1):
        return (2.0 / (ia0 + ia1)) * (p1 - p0)

    first, closing = [], []
    for cc in groups:
        at = col_of[cc]
        ia_top, ia_end = look(tab_ia, cN[0, :, at]), look(tab_ia, cN[RI - 1, :, at])
        t = flux(ia_end, pltpu.roll(ia_top, 7, 0), pN[RI - 1, :, at], pltpu.roll(pN[0, :, at], 7, 0))
        closing.append(jnp.where(sub < 7, t, 0.0))
        first += [pltpu.roll(closing[cc], 1, 0), ia_top]

    def flow_row(i, carry):
        new = []
        for cc in groups:
            at = col_of[cc]
            nxt = look(tab_ia, cN[i + 1, :, at])
            t = flux(carry[2 * cc + 1], nxt, pN[i, :, at], pN[i + 1, :, at])
            uN[i, :, at] = sN[i, :, at] + 0.2 * (t - carry[2 * cc])
            new += [t, nxt]
        return tuple(new)

    before = lax.fori_loop(0, RI - 1, flow_row, tuple(first))
    for cc in groups:
        at = col_of[cc]
        uN[RI - 1, :, at] = sN[RI - 1, :, at] + 0.2 * (closing[cc] - before[2 * cc])

    def level_t():
        blocks(lambda g, cc: put_t(uT, g, cc, (block_of(uN, g, cc) + block_of(prN, g, cc)).T))

    level_t()

    flows = []
    for q, g in chains:
        if q == 0:
            t = flux(
                iaT[g, row8(CJ - 1), :], pltpu.roll(iaT[g, row8(0), :], 7, 0),
                pT[g, row8(CJ - 1), :], pltpu.roll(pT[g, row8(0), :], 7, 0),
            )
            flows.append(pltpu.roll(jnp.where(sub < 7, t, 0.0), 1, 0))
        else:
            at, nxt = row8(q * QL - 1), row8(q * QL)
            flows.append(flux(iaT[g, at, :], iaT[g, nxt, :], pT[g, at, :], pT[g, nxt, :]))
    ends_of = [pltpu.roll(flows[g], 7, 0) for g in range(2)]
    ends_of = [jnp.where(sub < 7, t, 0.0) for t in ends_of]

    def source_cell(g, at, t, before, f, sum_c):
        d = t - before
        dT[g, at, :] = d
        value = pT[g, at, :] - 0.2 * (uT[g, at, :] + 0.2 * d)
        rate = rT[g, at, :]
        value = (1.0 - rate) * value
        return value + rate * f, sum_c + value * HcT[g, at, :]

    def source_row(i, carry):
        new = []
        for n, (q, g) in enumerate(chains):
            t0, f, sum_c = carry[3 * n : 3 * n + 3]
            at, nxt = row8(q * QL + i), row8(q * QL + i + 1)
            t = flux(iaT[g, at, :], iaT[g, nxt, :], pT[g, at, :], pT[g, nxt, :])
            new += [t, *source_cell(g, at, t, t0, f, sum_c)]
        return tuple(new)

    init = []
    for n in range(8):
        init += [flows[n], zero, zero]
    sums = lax.fori_loop(0, QL - 1, source_row, tuple(init))
    line_b, line_c = [zero, zero], [zero, zero]
    for n, (q, g) in enumerate(chains):
        t = ends_of[g] if q == QN - 1 else flows[n + 2]
        f, sum_c = source_cell(g, row8((q + 1) * QL - 1), t, *sums[3 * n : 3 * n + 3])
        left, right, turn = x_factors[g][q]
        line_b[g] = line_b[g] + f * right
        line_c[g] = line_c[g] + f * turn + sum_c * left
    line_b = [jnp.sum(x, axis=0, keepdims=True) for x in line_b]
    line_c = [jnp.sum(x, axis=0, keepdims=True) for x in line_c]

    def turn_back(g, cc):
        grow = get_t(GcT, g, cc) * get_t(rT, g, cc)
        bounce = get_t(HcT, g, cc) * get_t(rT, g, cc)
        full, turned = [], []
        for q in range(QN):
            left, right, turn = (xsc[g, q, k, pl.ds(cc, 1), :] for k in range(3))
            rows = slice(q * QL, (q + 1) * QL)
            full.append(grow[rows] * right)
            turned.append(grow[rows] * turn + bounce[rows] * left)
        for value, dst in ((full, GN), (turned, HN)):
            block = jnp.concatenate(value, axis=0).T
            dst[pl.ds(g * 16, 16), :, cols(cc)] = block.reshape(16, 8, LANES)

    blocks(turn_back)

    for cp in halo:
        cp.wait_recv()
    lane = lax.broadcasted_iota(jnp.int32, (1, LANES), 1)
    for n, (i, s, has) in enumerate(((0, 0, r > 0), (RI - 1, RS - 1, r < nrow - 1))):
        tot_b, tot_c = zero, zero
        here = jnp.logical_and(sub == s, has)
        for cc in groups:
            at = col_of[cc]
            code = cN[i, :, at]
            other = look(tab_ia, jnp.where(sub == s, hc[n, :, at], 0))
            q = flux(look(tab_ia, code), other, pN[i, :, at], hp[n, :, at])
            q = jnp.where(here, q, 0.0)
            uN[i, :, at] = uN[i, :, at] + 0.2 * q
            q = -0.04 * q * look(tab_w, code)
            tot_b = tot_b + q * GN[i, :, at]
            tot_c = tot_c + q * HN[i, :, at]
        mine = lane == (0 if n == 0 else LANES - 1)
        line_b[n] = line_b[n] + jnp.where(mine, jnp.sum(tot_b), 0.0)
        line_c[n] = line_c[n] + jnp.where(mine, jnp.sum(tot_c), 0.0)
    for g in range(2):
        lb[c, 0, pl.ds(g, 1), :] = line_b[g]
        lb[c, 1, pl.ds(g, 1), :] = line_c[g]
    late = [to_row(lb, l_send, l_recv, k) for k in range(1, ncol)]
    for cp in late:
        cp.start()

    def rates_row(i, carry):
        new = []
        for cc in groups:
            at = col_of[cc]
            rate = look(tab_r, cN[i, :, at])
            rN[i, :, at] = rate
            fN[i, :, at] = carry[cc]
            new.append(carry[cc] * rate)
        return tuple(new)

    ya = lax.fori_loop(0, RI, rates_row, (one,) * 8, unroll=2)

    def bounce_row(t, carry):
        i = RI - 1 - t
        new = []
        for cc in groups:
            at = col_of[cc]
            rate = rN[i, :, at]
            grow = carry[2 * cc]
            bounce = (1.0 - rate) * fN[i, :, at] + carry[2 * cc + 1]
            GyC[i, :, at] = grow
            HyC[i, :, at] = bounce
            new += [rate * grow, rate * bounce]
        return tuple(new)

    yd = lax.fori_loop(0, RI, bounce_row, (one, zero) * 8, unroll=2)[1::2]
    for cc in groups:
        factors, all_a, all_d = carry_factors([ya[cc]], [yd[cc]])
        for k in range(3):
            ysc[k, cc] = factors[0][k]
        yad[0, cc] = ya[cc]
        yad[1, cc] = yd[cc]
        ye[r, 0, pl.ds(cc, 1), :] = all_a[0:1]
        ye[r, 1, pl.ds(cc, 1), :] = all_d[0:1]
    y_early = [to_col(ye, ye_send, ye_recv, k) for k in range(1, nrow)]
    for cp in y_early:
        cp.start()

    level_t()

    def x_fwd(i, carry):
        new = []
        for n, (q, g) in enumerate(chains):
            at = row8(q * QL + i)
            rate = rT[g, at, :]
            value = pT[g, at, :] - 0.2 * (uT[g, at, :] + 0.2 * dT[g, at, :])
            f = (1.0 - rate) * value + rate * carry[n]
            fT[g, at, :] = f
            new.append(f)
        return tuple(new)

    xb = lax.fori_loop(0, QL, x_fwd, (zero,) * 8, unroll=2)

    def x_bwd(t, carry):
        i = QL - 1 - t
        new = []
        for n, (q, g) in enumerate(chains):
            at = row8(q * QL + i)
            rate = rT[g, at, :]
            b = (1.0 - rate) * fT[g, at, :] + rate * carry[n]
            sT[g, at, :] = b
            new.append(b)
        return tuple(new)

    xc = lax.fori_loop(0, QL, x_bwd, (zero,) * 8, unroll=2)
    for g in range(2):
        left, right = carry_values(
            xA[g], [xb[q * 2 + g] for q in range(QN)], [xc[q * 2 + g] for q in range(QN)], xD[g]
        )
        for q in range(QN):

            def fix(i, _, g=g, q=q, fl=left[q], br=right[q]):
                at = row8(q * QL + i)
                more = GcT[g, at, :] * br + HcT[g, at, :] * fl
                sT[g, at, :] = sT[g, at, :] + rT[g, at, :] * more
                return 0

            lax.fori_loop(0, QL, fix, 0, unroll=8)

    def solved_back(g, cc):
        bN[pl.ds(g * 16, 16), :, cols(cc)] = get_t(sT, g, cc).T.reshape(16, 8, LANES)

    blocks(solved_back)

    for cp in early:
        cp.wait_recv()
    nil = jnp.zeros((2, LANES), F32)
    faces = []
    for j in range(ncol - 1):
        faces.append(
            0.04 * flux(eb[j, 5], eb[j + 1, 4], eb[j, 3], eb[j + 1, 2])
        )
    into, gain, back, back_gain = [], [], [], []
    for j in range(ncol):
        r_w, r_e = eb[j, 6], eb[j, 7]
        west = faces[j - 1] if j > 0 else nil
        east = faces[j] if j < ncol - 1 else nil
        out_e = -(1.0 - r_e) * east
        into.append((1.0 - r_w) / r_w * west)
        turn_e = (1.0 - r_e) / r_e * out_e
        gain.append(eb[j, 0] * into[j] + out_e)
        back.append(turn_e)
        back_gain.append(eb[j, 0] * turn_e + eb[j, 1] * into[j])
    for cp in late:
        cp.wait_recv()
    f, fs = nil, []
    for j in range(ncol):
        fs.append(f)
        f = eb[j, 0] * f + (lb[j, 0] + gain[j])
    b = nil
    for j in reversed(range(ncol)):
        xin[j, 0] = fs[j] + into[j]
        xin[j, 1] = b + back[j]
        b = eb[j, 0] * b + (lb[j, 1] + back_gain[j] + eb[j, 1] * fs[j])
    for g in range(2):
        for src, dst in ((0, fB), (1, bB)):
            line = xin[c, src, pl.ds(g, 1), :]
            dst[pl.ds(g * 16, 16), :, :] = (
                jnp.broadcast_to(line, (LANES, LANES)).T.reshape(16, 8, LANES)
            )

    def solved_row(i, carry):
        new = []
        fb, bb = fB[i], bB[i]
        for cc in groups:
            at = col_of[cc]
            rate = rN[i, :, at]
            value = bN[i, :, at] + GN[i, :, at] * bb + HN[i, :, at] * fb
            value = (1.0 - rate) * value
            f = value + rate * carry[2 * cc]
            fN[i, :, at] = f
            new += [f, carry[2 * cc + 1] + value * HyC[i, :, at]]
        return tuple(new)

    sums = lax.fori_loop(0, RI, solved_row, (zero,) * 16, unroll=2)
    yb = sums[0::2]
    for cc in groups:
        left, right, turn = (ysc[k, cc] for k in range(3))
        sum_b = yb[cc] * right
        sum_c = yb[cc] * turn + sums[2 * cc + 1] * left
        yl[r, 0, pl.ds(cc, 1), :] = jnp.sum(sum_b, axis=0, keepdims=True)
        yl[r, 1, pl.ds(cc, 1), :] = jnp.sum(sum_c, axis=0, keepdims=True)
    y_late = [to_col(yl, yl_send, yl_recv, k) for k in range(1, nrow)]
    for cp in y_late:
        cp.start()

    def y_bwd(t, carry):
        i = RI - 1 - t
        new = []
        for cc in groups:
            at = col_of[cc]
            rate = rN[i, :, at]
            b = (1.0 - rate) * fN[i, :, at] + rate * carry[cc]
            xN[i, :, at] = b
            new.append(b)
        return tuple(new)

    yc = lax.fori_loop(0, RI, y_bwd, (zero,) * 8, unroll=2)
    for cc in groups:
        left, right = carry_values([yad[0, cc]], [yb[cc]], [yc[cc]], [yad[1, cc]])
        yfx[0, cc] = left[0]
        yfx[1, cc] = right[0]

    edge_w = jnp.where(c > 0, 1.0, 0.0)
    edge_e = jnp.where(c < ncol - 1, 1.0, 0.0)
    low, high = lax.rem(c + ncol - 1, ncol), lax.rem(c + 1, ncol)
    q_w = flux(eb[c, 4], eb[low, 5], eb[c, 2], eb[low, 3]) * edge_w
    q_e = flux(eb[c, 5], eb[high, 4], eb[c, 3], eb[high, 2]) * edge_e
    for g in range(2):
        dT[g, pl.ds(0, 1), :] = dT[g, pl.ds(0, 1), :] + q_w[g : g + 1]
        dT[g, pl.ds(last, 1), :] = dT[g, pl.ds(last, 1), :] + q_e[g : g + 1]

    def surface_back(g, cc):
        at = (pl.ds(g * 16, 16), slice(None), cols(cc))
        snN[at] = uN[at] + 0.2 * get_t(dT, g, cc).T.reshape(16, 8, LANES)

    blocks(surface_back)

    for cp in y_early:
        cp.wait_recv()
    for cp in y_late:
        cp.wait_recv()
    f = zero
    fs = []
    for j in range(nrow):
        fs.append(f)
        f = ye[j, 0] * f + yl[j, 0]
    b = zero
    own_f, own_b = zero, zero
    for j in reversed(range(nrow)):
        own_f = jnp.where(r == j, fs[j], own_f)
        own_b = jnp.where(r == j, b, own_b)
        b = ye[j, 0] * b + (yl[j, 1] + ye[j, 1] * fs[j])
    for cc in groups:
        left, right, turn = (ysc[k, cc] for k in range(3))
        f_row = jnp.broadcast_to(own_f[cc : cc + 1], (8, LANES))
        b_row = jnp.broadcast_to(own_b[cc : cc + 1], (8, LANES))
        inflow[0, cc] = yfx[0, cc] + left * f_row
        inflow[1, cc] = yfx[1, cc] + right * b_row + turn * f_row
    for cp in halo + early + late + y_early + y_late:
        cp.wait_send()


def finish(snN, xN, rN, GyC, HyC, inflow, sn_h, out_h, oN, sem):
    def store(src, dst, k, half):
        rows = pl.ds(half * 16, 16)
        return [
            pltpu.make_async_copy(src.at[rows, s, :], dst.at[s, rows, :], sem.at[k, half, s])
            for s in range(RS)
        ]

    copies = store(snN, sn_h, 0, 0) + store(snN, sn_h, 0, 1)
    for cp in copies:
        cp.start()
    groups = range(CC)
    left = [inflow[0, cc] for cc in groups]
    right = [inflow[1, cc] for cc in groups]

    def last_row(i, _):
        for cc in groups:
            at = pl.ds(cc * LANES, LANES)
            more = GyC[i, :, at] * right[cc] + HyC[i, :, at] * left[cc]
            oN[i, :, at] = xN[i, :, at] + rN[i, :, at] * more
        return 0

    for half in range(2):
        lax.fori_loop(half * 16, half * 16 + 16, last_row, 0, unroll=2)
        new = store(oN, out_h, 1, half)
        for cp in new:
            cp.start()
        copies += new
    for cp in copies:
        cp.wait()


def shards(nrow, ncol, surface, potential, depth_codes, class_depth, class_length, ship_rows,
           ship_cols, ship_reach, ship_strength):
    tile = (RS, RI, COLS)
    natural = pltpu.VMEM((RI, RS, COLS), F32)
    turned = pltpu.VMEM((2, CJ * CC, LANES), F32)
    dma = pltpu.SemaphoreType.DMA
    hbm = pl.BlockSpec(memory_space=pl.ANY)
    vmem = pl.BlockSpec(memory_space=pltpu.VMEM)
    held = pl.pallas_call(
        functools.partial(kernel, nrow, ncol),
        out_shape=[natural] * 5 + [pltpu.VMEM((2, CC, 8, LANES), F32)],
        in_specs=[hbm] * 9,
        out_specs=[vmem] * 6,
        scratch_shapes=[pltpu.VMEM((RI, RS, COLS), jnp.int32)]
        + [natural] * 8
        + [turned] * 9
        + [
            pltpu.VMEM((RI, RS, LANES), F32),
            pltpu.VMEM((RI, RS, LANES), F32),
            pltpu.VMEM((2, 8, COLS), F32),
            pltpu.VMEM((2, 8, COLS), jnp.int32),
            pltpu.VMEM((ncol, 8, 2, LANES), F32),
            pltpu.VMEM((ncol, 2, 2, LANES), F32),
            pltpu.VMEM((nrow, 2, 8, LANES), F32),
            pltpu.VMEM((nrow, 2, 8, LANES), F32),
            pltpu.VMEM((ncol, 2, 2, LANES), F32),
            pltpu.VMEM((2, QN, 3, 8, LANES), F32),
            pltpu.VMEM((3, CC, 8, LANES), F32),
            pltpu.VMEM((2, CC, 8, LANES), F32),
            pltpu.VMEM((2, CC, 8, LANES), F32),
            *[pltpu.SMEM((8,), F32)] * 2,
            *[pltpu.SMEM((SHIPS,), jnp.int32)] * 3,
            pltpu.SMEM((SHIPS,), F32),
            dma((6,)),
            dma((3, RS)), dma((2, 2)), dma((2, 2)),
            dma((ncol,)), dma((ncol,)), dma((ncol,)), dma((ncol,)),
            dma((nrow,)), dma((nrow,)), dma((nrow,)), dma((nrow,)),
        ],
        compiler_params=pltpu.CompilerParams(
            collective_id=0, has_side_effects=True, vmem_limit_bytes=32 * 1024 * 1024
        ),
    )(
        *[
            pltpu.with_memory_space_constraint(x, pltpu.HBM)
            for x in (
                class_depth, class_length, ship_rows, ship_cols, ship_reach, ship_strength,
                potential.reshape(tile), depth_codes.reshape(tile), surface.reshape(tile),
            )
        ]
    )
    surface_next, potential_next = pl.pallas_call(
        finish,
        out_shape=[jax.ShapeDtypeStruct(tile, F32)] * 2,
        in_specs=[vmem] * 6,
        out_specs=[hbm] * 2,
        scratch_shapes=[natural, dma((2, 2, RS))],
        compiler_params=pltpu.CompilerParams(vmem_limit_bytes=16 * 1024 * 1024),
    )(*held)
    return surface_next.reshape(ROWS, COLS), potential_next.reshape(ROWS, COLS)


def solution(mesh):
    in_specs = (P("row", "col"), P("row", "col"), P("row", "col"), P(), P(), P(), P(), P(), P())
    out_specs = (P("row", "col"), P("row", "col"))
    return jax.shard_map(
        functools.partial(shards, mesh.shape["row"], mesh.shape["col"]),
        mesh=mesh, in_specs=in_specs, out_specs=out_specs, check_vma=False,
    )
```

```python
import functools

import jax
import jax.numpy as jnp
from jax import lax
from jax.experimental import pallas as pl
from jax.experimental.pallas import tpu as pltpu
from jax.sharding import PartitionSpec as P

MESH = pl.DeviceIdType.MESH
F32 = jnp.float32
ROWS, COLS = 256, 1024
RI, RS = 32, 8
CJ, CC = 128, 8
QN, QL = 4, 32
LANES = 128
SHIPS = 32


def sub_iota():
    return lax.broadcasted_iota(jnp.int32, (8, LANES), 0)


def wide_iota(width):
    return lax.broadcasted_iota(jnp.int32, (8, width), 0)


def from_before(x, k, fill):
    return jnp.where(wide_iota(x.shape[1]) >= k, pltpu.roll(x, k, 0), fill)


def from_after(x, k, fill):
    return jnp.where(wide_iota(x.shape[1]) < 8 - k, pltpu.roll(x, 8 - k, 0), fill)


def prefix_pair(a, b):
    for k in (1, 2, 4):
        b = a * from_before(b, k, 0.0) + b
        a = a * from_before(a, k, 1.0)
    return a, b


def suffix_pair(a, c):
    for k in (1, 2, 4):
        c = c + a * from_after(c, k, 0.0)
        a = a * from_after(a, k, 1.0)
    return a, c


def suffix_bounce(a, d):
    for k in (1, 2, 4):
        d = d + a * from_after(d, k, 0.0) * a
        a = a * from_after(a, k, 1.0)
    return a, d


def carry_factors(a, d):
    count = len(a)
    after_a, after_d = [None] * count, [None] * count
    run_a, run_d = jnp.ones_like(a[0]), jnp.zeros_like(a[0])
    for q in reversed(range(count)):
        after_a[q], after_d[q] = run_a, run_d
        run_d = d[q] + a[q] * run_d * a[q]
        run_a = a[q] * run_a
    before = jnp.ones_like(run_a)
    for k in (1,):
        inclusive, _ = prefix_pair(run_a, jnp.zeros_like(run_a))
        before = from_before(inclusive, k, 1.0)
    all_a, all_d = suffix_bounce(run_a, run_d)
    out_a, out_d = from_after(all_a, 1, 1.0), from_after(all_d, 1, 0.0)
    result = []
    for q in range(count):
        right_a = out_a * after_a[q]
        right_d = after_d[q] + after_a[q] * out_d * after_a[q]
        result.append((before, right_a, before * a[q] * right_d))
        before = before * a[q]
    return result, all_a, all_d


def carry_values(a, b, c, d):
    count = len(a)
    run_a, run_b = a[0], b[0]
    for q in range(1, count):
        run_b = a[q] * run_b + b[q]
        run_a = a[q] * run_a
    _, inclusive = prefix_pair(run_a, run_b)
    left = [from_before(inclusive, 1, 0.0)]
    for q in range(count - 1):
        left.append(a[q] * left[q] + b[q])
    c = [c[q] + d[q] * left[q] for q in range(count)]
    run_c = c[count - 1]
    for q in reversed(range(count - 1)):
        run_c = c[q] + a[q] * run_c
    _, inclusive = suffix_pair(run_a, run_c)
    right = [None] * count
    right[count - 1] = from_after(inclusive, 1, 0.0)
    for q in reversed(range(1, count)):
        right[q - 1] = a[q] * right[q] + c[q]
    return left, right


def total(terms):
    while len(terms) > 1:
        terms = [
            terms[k] + terms[k + 1] if k + 1 < len(terms) else terms[k]
            for k in range(0, len(terms), 2)
        ]
    return terms[0]


def weights(a, d, me, ref):
    count = len(a)
    zero, one = jnp.zeros_like(a[0]), jnp.ones_like(a[0])
    run, from_c = zero, []
    for j in range(count):
        from_c.append(run)
        ref[j, 1] = run
        run = jnp.where(me == j, one, run * a[j])
    left, right = zero, zero
    for j in reversed(range(count)):
        ref[j, 0] = left
        ref[j, 2] = right
        left = jnp.where(me == j, one, left * a[j])
        right = from_c[j] * d[j] + a[j] * right


def kernel(
    nrow,
    ncol,
    depth_h, length_h, srow_h, scol_h, sreach_h, sstr_h,
    pot_h, code_h, surf_h,
    snN, xN, rN, GyC, HyC, inflow,
    cN, pN, sN, prN, uN, GN, HN, bN, fN,
    rT, iaT, pT, uT, GcT, HcT, dT, sT, fT,
    fB, bB, hp, hc,
    eb, lb, ye, yl, xin, xsc, ysc, yad, yfx, xw, yw,
    depth_s, length_s, srow_s, scol_s, sreach_s, sstr_s, s_sem,
    in_sem, h_send, h_recv, e_send, e_recv, l_send, l_recv,
    ye_send, ye_recv, yl_send, yl_recv,
):
    r = lax.axis_index("row")
    c = lax.axis_index("col")

    def loads(src, dst, k):
        return [
            pltpu.make_async_copy(src.at[s], dst.at[:, s, :], in_sem.at[k, s]) for s in range(RS)
        ]

    code_in = loads(code_h, cN, 0)
    pot_in = loads(pot_h, pN, 1)
    surf_in = loads(surf_h, sN, 2)
    small = [
        pltpu.make_async_copy(src, dst, s_sem.at[k])
        for k, (src, dst) in enumerate(
            (
                (depth_h, depth_s), (length_h, length_s), (srow_h, srow_s),
                (scol_h, scol_s), (sreach_h, sreach_s), (sstr_h, sstr_s),
            )
        )
    ]
    for cp in small + code_in + pot_in + surf_in:
        cp.start()

    barrier = pltpu.get_barrier_semaphore()
    north, south = lax.rem(r + nrow - 1, nrow), lax.rem(r + 1, nrow)
    for k in [1, nrow - 1] + list(range(2, nrow - 1)):
        pl.semaphore_signal(
            barrier, inc=1, device_id=(lax.rem(r + k, nrow), c), device_id_type=MESH
        )
    for k in range(1, ncol):
        pl.semaphore_signal(
            barrier, inc=1, device_id=(r, lax.rem(c + k, ncol)), device_id_type=MESH
        )

    for cp in small:
        cp.wait()
    sub = sub_iota()
    tab_len = jnp.zeros((8, LANES), F32)
    tab_dep = jnp.zeros((8, LANES), F32)
    for k in range(8):
        tab_len = jnp.where(sub == k, length_s[k], tab_len)
        tab_dep = jnp.where(sub == k, depth_s[k], tab_dep)
    tab_r = jnp.exp(-1.0 / tab_len)
    tab_w = 1.0 / tab_r
    tab_ia = 1.0 / tab_dep

    def look(tab, idx):
        return jnp.take_along_axis(tab, idx, axis=0)

    params = []
    for k in range(0, SHIPS, 8):
        rows, cols_of, wide, strong = (jnp.zeros((8, LANES), d) for d in (jnp.int32,) * 2 + (F32,) * 2)
        for n in range(8):
            rows = jnp.where(sub == n, srow_s[k + n], rows)
            cols_of = jnp.where(sub == n, scol_s[k + n], cols_of)
            wide = jnp.where(sub == n, (sreach_s[k + n] + 1).astype(F32), wide)
            strong = jnp.where(sub == n, sstr_s[k + n], strong)
        params.append((rows, cols_of, 1.0 / wide, strong))
    lane8 = lax.broadcasted_iota(jnp.int32, (8, LANES), 1)

    def near(at, centre, narrow):
        return jnp.maximum(0.0, 1.0 - jnp.abs(at - centre).astype(F32) * narrow)

    def parts_of(x):
        high = x.astype(jnp.bfloat16).astype(F32)
        rest = x - high
        mid = rest.astype(jnp.bfloat16).astype(F32)
        return high, mid, rest - mid

    pad = jnp.zeros((64, LANES), F32)
    along_y = []
    for g in range(2):
        held = lane8 + g * LANES
        y = r * ROWS + lax.bitwise_and(held, 7) * RI + lax.shift_right_logical(held, 3)
        h, m, l = parts_of(jnp.concatenate([near(y, p[0], p[2]) * p[3] for p in params], axis=0))
        deep = jnp.concatenate([h, h, m, m, h, l, pad], axis=0)
        along_y.append(
            jnp.concatenate([deep[:LANES].T, deep[LANES:].T], axis=1).astype(jnp.bfloat16)
        )
    along_y = jnp.concatenate(along_y, axis=0)
    for cc in range(0, CC, 2):
        wide = []
        for k in range(2):
            x = c * COLS + (cc + k) * LANES + lane8
            h, m, l = parts_of(jnp.concatenate([near(x, p[1], p[2]) for p in params], axis=0))
            wide.append(jnp.concatenate([h, m, h, m, l, h, pad], axis=0).astype(jnp.bfloat16))
        block = jnp.dot(
            along_y, jnp.concatenate(wide, axis=1), preferred_element_type=F32
        )
        prN[:, :, pl.ds(cc * LANES, 2 * LANES)] = block.reshape(RI, RS, 2 * LANES)

    for cp in code_in:
        cp.wait()

    def cols(cc):
        return pl.ds(pl.multiple_of(cc * LANES, LANES), LANES)

    def block_of(ref, g, cc):
        return ref[pl.ds(g * 16, 16), :, cols(cc)].reshape(LANES, LANES)

    def put_t(ref, g, cc, value):
        ref.at[g][pl.ds(cc, CJ, stride=CC), :] = value

    def get_t(ref, g, cc):
        return ref.at[g][pl.ds(cc, CJ, stride=CC), :]

    def blocks(body):
        @pl.loop(0, CC, unroll=8)
        def _(cc):
            for g in range(2):
                body(g, cc)

    def codes_block(g, cc):
        idx = block_of(cN, g, cc).T.reshape(16, 8, LANES)
        for tab, ref in ((tab_r, rT), (tab_ia, iaT)):
            put_t(ref, g, cc, jnp.concatenate([look(tab, idx[k]) for k in range(16)], axis=0))

    blocks(codes_block)

    def row8(j):
        return pl.ds(pl.multiple_of(j * 8, 8), 8)

    for cp in pot_in:
        cp.wait()
    pl.semaphore_wait(barrier, nrow - 1 + ncol - 1)
    halo = []
    for n, (src_i, src_s, dst_s, target) in enumerate(
        ((RI - 1, RS - 1, 0, south), (0, 0, RS - 1, north))
    ):
        for m, (src, dst) in enumerate(((pN, hp), (cN, hc))):
            halo.append(
                pltpu.make_async_remote_copy(
                    src_ref=src.at[src_i, pl.ds(src_s, 1), :],
                    dst_ref=dst.at[n, pl.ds(dst_s, 1), :],
                    send_sem=h_send.at[n, m],
                    recv_sem=h_recv.at[n, m],
                    device_id=(target, c),
                    device_id_type=MESH,
                )
            )
    for cp in halo:
        cp.start()

    one = jnp.ones((8, LANES), F32)
    zero = jnp.zeros((8, LANES), F32)
    chains = [(q, g) for q in range(QN) for g in range(2)]

    def fwd(i, carry):
        new = []
        for n, (q, g) in enumerate(chains):
            at = row8(q * QL + i)
            fT[g, at, :] = carry[n]
            new.append(carry[n] * rT[g, at, :])
        return tuple(new)

    xa = lax.fori_loop(0, QL, fwd, (one,) * 8, unroll=4)

    def bwd(t, carry):
        i = QL - 1 - t
        new = []
        for n, (q, g) in enumerate(chains):
            at = row8(q * QL + i)
            rate = rT[g, at, :]
            grow = carry[2 * n]
            bounce = (1.0 - rate) * fT[g, at, :] + carry[2 * n + 1]
            GcT[g, at, :] = grow
            HcT[g, at, :] = bounce
            new += [rate * grow, rate * bounce]
        return tuple(new)

    ends = lax.fori_loop(0, QL, bwd, (one, zero) * 8, unroll=2)
    xd = ends[1::2]
    xA = [[xa[q * 2 + g] for q in range(QN)] for g in range(2)]
    xD = [[xd[q * 2 + g] for q in range(QN)] for g in range(2)]
    line_a, line_d, x_factors = [], [], []
    for g in range(2):
        factors, all_a, all_d = carry_factors(xA[g], xD[g])
        line_a.append(all_a[0:1])
        line_d.append(all_d[0:1])
        x_factors.append(factors)
        for q in range(QN):
            for k in range(3):
                xsc[g, q, k] = factors[q][k]


    blocks(lambda g, cc: put_t(pT, g, cc, block_of(pN, g, cc).T))

    last = CJ * CC - 1
    for g in range(2):
        eb[c, 0, pl.ds(g, 1), :] = line_a[g]
        eb[c, 1, pl.ds(g, 1), :] = line_d[g]
        eb[c, 2, pl.ds(g, 1), :] = pT[g, pl.ds(0, 1), :]
        eb[c, 3, pl.ds(g, 1), :] = pT[g, pl.ds(last, 1), :]
        eb[c, 4, pl.ds(g, 1), :] = iaT[g, pl.ds(0, 1), :]
        eb[c, 5, pl.ds(g, 1), :] = iaT[g, pl.ds(last, 1), :]
        eb[c, 6, pl.ds(g, 1), :] = rT[g, pl.ds(0, 1), :]
        eb[c, 7, pl.ds(g, 1), :] = rT[g, pl.ds(last, 1), :]

    row_peers = sorted(
        ((dx, dy, dc) for dx in range(4) for dy in range(2) for dc in range(2)),
        key=lambda o: -(min(o[0], 4 - o[0]) + 2 * o[1]),
    )
    row_peers = [o for o in row_peers if any(o)]
    col_peers = sorted(
        ((dz, dy) for dz in range(4) for dy in range(2)), key=lambda o: -(min(o[0], 4 - o[0]) + o[1])
    )
    col_peers = [o for o in col_peers if any(o)]

    def to_row(buf, send, recv, k):
        dx, dy, dc = row_peers[k]
        x, y, core = lax.div(c, 4), lax.rem(lax.div(c, 2), 2), lax.rem(c, 2)
        peer = lax.rem(x + dx, 4) * 4 + lax.rem(y + dy, 2) * 2 + lax.rem(core + dc, 2)
        return pltpu.make_async_remote_copy(
            src_ref=buf.at[c],
            dst_ref=buf.at[c],
            send_sem=send,
            recv_sem=recv,
            device_id=(r, peer),
            device_id_type=MESH,
        )

    def to_col(buf, send, recv, k):
        dz, dy = col_peers[k]
        z, y = lax.div(r, 2), lax.rem(r, 2)
        peer = lax.rem(z + dz, 4) * 2 + lax.rem(y + dy, 2)
        return pltpu.make_async_remote_copy(
            src_ref=buf.at[r],
            dst_ref=buf.at[r],
            send_sem=send,
            recv_sem=recv,
            device_id=(peer, c),
            device_id_type=MESH,
        )

    def wait_all(buf, sem, count):
        rest = buf.at[pl.ds(0, count - 1)]
        pltpu.make_async_copy(rest, rest, sem).wait()

    early = [to_row(eb, e_send, e_recv, k) for k in range(ncol - 1)]
    for cp in early:
        cp.start()

    for cp in surf_in:
        cp.wait()

    groups = range(CC)
    col_of = [pl.ds(cc * LANES, LANES) for cc in groups]

    def flux(ia0, ia1, p0, p1):
        return (2.0 / (ia0 + ia1)) * (p1 - p0)

    first, closing = [], []
    for cc in groups:
        at = col_of[cc]
        ia_top, ia_end = look(tab_ia, cN[0, :, at]), look(tab_ia, cN[RI - 1, :, at])
        t = flux(ia_end, pltpu.roll(ia_top, 7, 0), pN[RI - 1, :, at], pltpu.roll(pN[0, :, at], 7, 0))
        closing.append(jnp.where(sub < 7, t, 0.0))
        first += [pltpu.roll(closing[cc], 1, 0), ia_top]

    def flow_row(i, carry):
        new = []
        for cc in groups:
            at = col_of[cc]
            nxt = look(tab_ia, cN[i + 1, :, at])
            t = flux(carry[2 * cc + 1], nxt, pN[i, :, at], pN[i + 1, :, at])
            uN[i, :, at] = sN[i, :, at] + 0.2 * (t - carry[2 * cc])
            new += [t, nxt]
        return tuple(new)

    before = lax.fori_loop(0, RI - 1, flow_row, tuple(first))
    for cc in groups:
        at = col_of[cc]
        uN[RI - 1, :, at] = sN[RI - 1, :, at] + 0.2 * (closing[cc] - before[2 * cc])

    def level_t():
        blocks(lambda g, cc: put_t(uT, g, cc, (block_of(uN, g, cc) + block_of(prN, g, cc)).T))

    level_t()

    flows = []
    for q, g in chains:
        if q == 0:
            t = flux(
                iaT[g, row8(CJ - 1), :], pltpu.roll(iaT[g, row8(0), :], 7, 0),
                pT[g, row8(CJ - 1), :], pltpu.roll(pT[g, row8(0), :], 7, 0),
            )
            flows.append(pltpu.roll(jnp.where(sub < 7, t, 0.0), 1, 0))
        else:
            at, nxt = row8(q * QL - 1), row8(q * QL)
            flows.append(flux(iaT[g, at, :], iaT[g, nxt, :], pT[g, at, :], pT[g, nxt, :]))
    ends_of = [pltpu.roll(flows[g], 7, 0) for g in range(2)]
    ends_of = [jnp.where(sub < 7, t, 0.0) for t in ends_of]

    def source_cell(g, at, t, before, f, sum_c):
        d = t - before
        dT[g, at, :] = d
        value = pT[g, at, :] - 0.2 * (uT[g, at, :] + 0.2 * d)
        rate = rT[g, at, :]
        value = (1.0 - rate) * value
        return value + rate * f, sum_c + value * HcT[g, at, :]

    def source_row(i, carry):
        new = []
        for n, (q, g) in enumerate(chains):
            t0, f, sum_c = carry[3 * n : 3 * n + 3]
            at, nxt = row8(q * QL + i), row8(q * QL + i + 1)
            t = flux(iaT[g, at, :], iaT[g, nxt, :], pT[g, at, :], pT[g, nxt, :])
            new += [t, *source_cell(g, at, t, t0, f, sum_c)]
        return tuple(new)

    init = []
    for n in range(8):
        init += [flows[n], zero, zero]
    sums = lax.fori_loop(0, QL - 1, source_row, tuple(init))
    line_b, line_c = [zero, zero], [zero, zero]
    for n, (q, g) in enumerate(chains):
        t = ends_of[g] if q == QN - 1 else flows[n + 2]
        f, sum_c = source_cell(g, row8((q + 1) * QL - 1), t, *sums[3 * n : 3 * n + 3])
        left, right, turn = x_factors[g][q]
        line_b[g] = line_b[g] + f * right
        line_c[g] = line_c[g] + f * turn + sum_c * left
    line_b = [jnp.sum(x, axis=0, keepdims=True) for x in line_b]
    line_c = [jnp.sum(x, axis=0, keepdims=True) for x in line_c]

    def turn_back(g, cc):
        rate = get_t(rT, g, cc)
        rate = rate * (1.0 - rate)
        grow = get_t(GcT, g, cc) * rate
        bounce = get_t(HcT, g, cc) * rate
        full, turned = [], []
        for q in range(QN):
            left, right, turn = (xsc[g, q, k, pl.ds(cc, 1), :] for k in range(3))
            rows = slice(q * QL, (q + 1) * QL)
            full.append(grow[rows] * right)
            turned.append(grow[rows] * turn + bounce[rows] * left)
        for value, dst in ((full, GN), (turned, HN)):
            block = jnp.concatenate(value, axis=0).T
            dst[pl.ds(g * 16, 16), :, cols(cc)] = block.reshape(16, 8, LANES)

    blocks(turn_back)

    for cp in halo:
        cp.wait_recv()
    lane = lax.broadcasted_iota(jnp.int32, (1, LANES), 1)
    for n, (i, s, has) in enumerate(((0, 0, r > 0), (RI - 1, RS - 1, r < nrow - 1))):
        tot_b, tot_c = zero, zero
        here = jnp.logical_and(sub == s, has)
        for cc in groups:
            at = col_of[cc]
            code = cN[i, :, at]
            other = look(tab_ia, jnp.where(sub == s, hc[n, :, at], 0))
            q = flux(look(tab_ia, code), other, pN[i, :, at], hp[n, :, at])
            q = jnp.where(here, q, 0.0)
            uN[i, :, at] = uN[i, :, at] + 0.2 * q
            q = -0.04 * q * look(tab_w, code)
            tot_b = tot_b + q * GN[i, :, at]
            tot_c = tot_c + q * HN[i, :, at]
        mine = lane == (0 if n == 0 else LANES - 1)
        line_b[n] = line_b[n] + jnp.where(mine, jnp.sum(tot_b), 0.0)
        line_c[n] = line_c[n] + jnp.where(mine, jnp.sum(tot_c), 0.0)
    for g in range(2):
        lb[c, 0, pl.ds(g, 1), :] = line_b[g]
        lb[c, 1, pl.ds(g, 1), :] = line_c[g]
    late = [to_row(lb, l_send, l_recv, k) for k in range(ncol - 1)]
    for cp in late:
        cp.start()

    def rates_row(i, carry):
        new = []
        for cc in groups:
            at = col_of[cc]
            rate = look(tab_r, cN[i, :, at])
            rN[i, :, at] = rate
            fN[i, :, at] = carry[cc]
            new.append(carry[cc] * rate)
        return tuple(new)

    ya = lax.fori_loop(0, RI, rates_row, (one,) * 8, unroll=2)

    def bounce_row(t, carry):
        i = RI - 1 - t
        new = []
        for cc in groups:
            at = col_of[cc]
            rate = rN[i, :, at]
            grow = carry[2 * cc]
            bounce = (1.0 - rate) * fN[i, :, at] + carry[2 * cc + 1]
            GyC[i, :, at] = grow
            HyC[i, :, at] = bounce
            new += [rate * grow, rate * bounce]
        return tuple(new)

    yd = lax.fori_loop(0, RI, bounce_row, (one, zero) * 8, unroll=2)[1::2]
    for cc in groups:
        factors, all_a, all_d = carry_factors([ya[cc]], [yd[cc]])
        for k in range(3):
            ysc[k, cc] = factors[0][k]
        yad[0, cc] = ya[cc]
        yad[1, cc] = yd[cc]
        ye[r, 0, pl.ds(cc, 1), :] = all_a[0:1]
        ye[r, 1, pl.ds(cc, 1), :] = all_d[0:1]
    y_early = [to_col(ye, ye_send, ye_recv, k) for k in range(nrow - 1)]
    for cp in y_early:
        cp.start()

    level_t()

    def x_fwd(i, carry):
        new = []
        for n, (q, g) in enumerate(chains):
            at = row8(q * QL + i)
            rate = rT[g, at, :]
            value = pT[g, at, :] - 0.2 * (uT[g, at, :] + 0.2 * dT[g, at, :])
            f = (1.0 - rate) * value + rate * carry[n]
            fT[g, at, :] = f
            new.append(f)
        return tuple(new)

    xb = lax.fori_loop(0, QL, x_fwd, (zero,) * 8, unroll=2)

    def x_bwd(t, carry):
        i = QL - 1 - t
        new = []
        for n, (q, g) in enumerate(chains):
            at = row8(q * QL + i)
            rate = rT[g, at, :]
            b = (1.0 - rate) * fT[g, at, :] + rate * carry[n]
            sT[g, at, :] = b
            new.append(b)
        return tuple(new)

    xc = lax.fori_loop(0, QL, x_bwd, (zero,) * 8, unroll=2)
    for g in range(2):
        left, right = carry_values(
            xA[g], [xb[q * 2 + g] for q in range(QN)], [xc[q * 2 + g] for q in range(QN)], xD[g]
        )
        for q in range(QN):

            def fix(i, _, g=g, q=q, fl=left[q], br=right[q]):
                at = row8(q * QL + i)
                more = GcT[g, at, :] * br + HcT[g, at, :] * fl
                rate = rT[g, at, :]
                sT[g, at, :] = (1.0 - rate) * (sT[g, at, :] + rate * more)
                return 0

            lax.fori_loop(0, QL, fix, 0, unroll=8)

    def solved_back(g, cc):
        bN[pl.ds(g * 16, 16), :, cols(cc)] = get_t(sT, g, cc).T.reshape(16, 8, LANES)

    blocks(solved_back)

    wait_all(eb, e_recv, ncol)
    nil = jnp.zeros((2, LANES), F32)
    faces = []
    for j in range(ncol - 1):
        faces.append(
            0.04 * flux(eb[j, 5], eb[j + 1, 4], eb[j, 3], eb[j + 1, 2])
        )
    into, gain, back, back_gain = [], [], [], []
    for j in range(ncol):
        r_w, r_e = eb[j, 6], eb[j, 7]
        west = faces[j - 1] if j > 0 else nil
        east = faces[j] if j < ncol - 1 else nil
        out_e = -(1.0 - r_e) * east
        into.append((1.0 - r_w) / r_w * west)
        turn_e = (1.0 - r_e) / r_e * out_e
        gain.append(eb[j, 0] * into[j] + out_e)
        back.append(turn_e)
        back_gain.append(eb[j, 0] * turn_e + eb[j, 1] * into[j])
    weights(
        [eb[j, 0] for j in range(ncol)], [eb[j, 1] for j in range(ncol)], c, xw
    )
    f_in, b_in = nil, nil
    for j in range(ncol):
        f_in = f_in + jnp.where(c == j, into[j], xw[j, 0] * gain[j])
        b_in = b_in + jnp.where(c == j, back[j], 0.0)
        b_in = b_in + xw[j, 1] * back_gain[j] + xw[j, 2] * gain[j]
    wait_all(lb, l_recv, ncol)
    f_in = f_in + total([xw[j, 0] * lb[j, 0] for j in range(ncol)])
    b_in = b_in + total([xw[j, 1] * lb[j, 1] + xw[j, 2] * lb[j, 0] for j in range(ncol)])
    xin[0] = f_in
    xin[1] = b_in
    for g in range(2):
        for src, dst in ((0, fB), (1, bB)):
            line = xin[src, pl.ds(g, 1), :]
            dst[pl.ds(g * 16, 16), :, :] = (
                jnp.broadcast_to(line, (LANES, LANES)).T.reshape(16, 8, LANES)
            )

    def solved_row(i, carry):
        new = []
        fb, bb = fB[i], bB[i]
        for cc in groups:
            at = col_of[cc]
            rate = rN[i, :, at]
            value = bN[i, :, at] + GN[i, :, at] * bb + HN[i, :, at] * fb
            f = value + rate * carry[2 * cc]
            fN[i, :, at] = f
            new += [f, carry[2 * cc + 1] + value * HyC[i, :, at]]
        return tuple(new)

    sums = lax.fori_loop(0, RI, solved_row, (zero,) * 16, unroll=4)
    yb = sums[0::2]
    for cc in groups:
        left, right, turn = (ysc[k, cc] for k in range(3))
        sum_b = yb[cc] * right
        sum_c = yb[cc] * turn + sums[2 * cc + 1] * left
        yl[r, 0, pl.ds(cc, 1), :] = jnp.sum(sum_b, axis=0, keepdims=True)
        yl[r, 1, pl.ds(cc, 1), :] = jnp.sum(sum_c, axis=0, keepdims=True)
    y_late = [to_col(yl, yl_send, yl_recv, k) for k in range(nrow - 1)]
    for cp in y_late:
        cp.start()

    def y_bwd(t, carry):
        i = RI - 1 - t
        new = []
        for cc in groups:
            at = col_of[cc]
            rate = rN[i, :, at]
            b = (1.0 - rate) * fN[i, :, at] + rate * carry[cc]
            xN[i, :, at] = b
            new.append(b)
        return tuple(new)

    yc = lax.fori_loop(0, RI, y_bwd, (zero,) * 8, unroll=2)
    for cc in groups:
        left, right = carry_values([yad[0, cc]], [yb[cc]], [yc[cc]], [yad[1, cc]])
        yfx[0, cc] = left[0]
        yfx[1, cc] = right[0]

    edge_w = jnp.where(c > 0, 1.0, 0.0)
    edge_e = jnp.where(c < ncol - 1, 1.0, 0.0)
    low, high = lax.rem(c + ncol - 1, ncol), lax.rem(c + 1, ncol)
    q_w = flux(eb[c, 4], eb[low, 5], eb[c, 2], eb[low, 3]) * edge_w
    q_e = flux(eb[c, 5], eb[high, 4], eb[c, 3], eb[high, 2]) * edge_e
    for g in range(2):
        dT[g, pl.ds(0, 1), :] = dT[g, pl.ds(0, 1), :] + q_w[g : g + 1]
        dT[g, pl.ds(last, 1), :] = dT[g, pl.ds(last, 1), :] + q_e[g : g + 1]

    def surface_back(g, cc):
        at = (pl.ds(g * 16, 16), slice(None), cols(cc))
        snN[at] = uN[at] + 0.2 * get_t(dT, g, cc).T.reshape(16, 8, LANES)

    blocks(surface_back)

    wait_all(ye, ye_recv, nrow)
    weights([ye[j, 0] for j in range(nrow)], [ye[j, 1] for j in range(nrow)], r, yw)
    for cp in halo:
        cp.wait_send()
    wait_all(eb, e_send, ncol)
    wait_all(lb, l_send, ncol)
    wait_all(ye, ye_send, nrow)
    wait_all(yl, yl_recv, nrow)
    own_f = total([yw[j, 0] * yl[j, 0] for j in range(nrow)])
    own_b = total([yw[j, 1] * yl[j, 1] + yw[j, 2] * yl[j, 0] for j in range(nrow)])
    for cc in groups:
        left, right, turn = (ysc[k, cc] for k in range(3))
        f_row = jnp.broadcast_to(own_f[cc : cc + 1], (8, LANES))
        b_row = jnp.broadcast_to(own_b[cc : cc + 1], (8, LANES))
        inflow[0, cc] = yfx[0, cc] + left * f_row
        inflow[1, cc] = yfx[1, cc] + right * b_row + turn * f_row
    wait_all(yl, yl_send, nrow)


def finish(snN, xN, rN, GyC, HyC, inflow, sn_h, out_h, oN, sem):
    def store(src, dst, k, half):
        rows = pl.ds(half * 16, 16)
        return [
            pltpu.make_async_copy(src.at[rows, s, :], dst.at[s, rows, :], sem.at[k, half, s])
            for s in range(RS)
        ]

    copies = store(snN, sn_h, 0, 0) + store(snN, sn_h, 0, 1)
    for cp in copies:
        cp.start()
    groups = range(CC)
    left = [inflow[0, cc] for cc in groups]
    right = [inflow[1, cc] for cc in groups]

    def last_row(i, _):
        for cc in groups:
            at = pl.ds(cc * LANES, LANES)
            more = GyC[i, :, at] * right[cc] + HyC[i, :, at] * left[cc]
            oN[i, :, at] = xN[i, :, at] + rN[i, :, at] * more
        return 0

    for half in range(2):
        lax.fori_loop(half * 16, half * 16 + 16, last_row, 0, unroll=2)
        new = store(oN, out_h, 1, half)
        for cp in new:
            cp.start()
        copies += new
    for cp in copies:
        cp.wait()


def shards(nrow, ncol, surface, potential, depth_codes, class_depth, class_length, ship_rows,
           ship_cols, ship_reach, ship_strength):
    tile = (RS, RI, COLS)
    natural = pltpu.VMEM((RI, RS, COLS), F32)
    turned = pltpu.VMEM((2, CJ * CC, LANES), F32)
    dma = pltpu.SemaphoreType.DMA
    hbm = pl.BlockSpec(memory_space=pl.ANY)
    vmem = pl.BlockSpec(memory_space=pltpu.VMEM)
    held = pl.pallas_call(
        functools.partial(kernel, nrow, ncol),
        out_shape=[natural] * 5 + [pltpu.VMEM((2, CC, 8, LANES), F32)],
        in_specs=[hbm] * 9,
        out_specs=[vmem] * 6,
        scratch_shapes=[pltpu.VMEM((RI, RS, COLS), jnp.int32)]
        + [natural] * 8
        + [turned] * 9
        + [
            pltpu.VMEM((RI, RS, LANES), F32),
            pltpu.VMEM((RI, RS, LANES), F32),
            pltpu.VMEM((2, 8, COLS), F32),
            pltpu.VMEM((2, 8, COLS), jnp.int32),
            pltpu.VMEM((ncol, 8, 2, LANES), F32),
            pltpu.VMEM((ncol, 2, 2, LANES), F32),
            pltpu.VMEM((nrow, 2, 8, LANES), F32),
            pltpu.VMEM((nrow, 2, 8, LANES), F32),
            pltpu.VMEM((2, 2, LANES), F32),
            pltpu.VMEM((2, QN, 3, 8, LANES), F32),
            pltpu.VMEM((3, CC, 8, LANES), F32),
            pltpu.VMEM((2, CC, 8, LANES), F32),
            pltpu.VMEM((2, CC, 8, LANES), F32),
            pltpu.VMEM((ncol, 3, 2, LANES), F32),
            pltpu.VMEM((nrow, 3, 8, LANES), F32),
            *[pltpu.SMEM((8,), F32)] * 2,
            *[pltpu.SMEM((SHIPS,), jnp.int32)] * 3,
            pltpu.SMEM((SHIPS,), F32),
            dma((6,)),
            dma((3, RS)), dma((2, 2)), dma((2, 2)),
            *[dma] * 8,
        ],
        compiler_params=pltpu.CompilerParams(
            collective_id=0, has_side_effects=True, vmem_limit_bytes=32 * 1024 * 1024
        ),
    )(
        *[
            pltpu.with_memory_space_constraint(x, pltpu.HBM)
            for x in (
                class_depth, class_length, ship_rows, ship_cols, ship_reach, ship_strength,
                potential.reshape(tile), depth_codes.reshape(tile), surface.reshape(tile),
            )
        ]
    )
    surface_next, potential_next = pl.pallas_call(
        finish,
        out_shape=[jax.ShapeDtypeStruct(tile, F32)] * 2,
        in_specs=[vmem] * 6,
        out_specs=[hbm] * 2,
        scratch_shapes=[natural, dma((2, 2, RS))],
        compiler_params=pltpu.CompilerParams(vmem_limit_bytes=16 * 1024 * 1024),
    )(*held)
    return surface_next.reshape(ROWS, COLS), potential_next.reshape(ROWS, COLS)


def solution(mesh):
    in_specs = (P("row", "col"), P("row", "col"), P("row", "col"), P(), P(), P(), P(), P(), P())
    out_specs = (P("row", "col"), P("row", "col"))
    return jax.shard_map(
        functools.partial(shards, mesh.shape["row"], mesh.shape["col"]),
        mesh=mesh, in_specs=in_specs, out_specs=out_specs, check_vma=False,
    )
```

```python
import functools

import jax
import jax.numpy as jnp
from jax import lax
from jax.experimental import pallas as pl
from jax.experimental.pallas import tpu as pltpu
from jax.sharding import PartitionSpec as P

MESH = pl.DeviceIdType.MESH
F32 = jnp.float32
ROWS, COLS = 256, 1024
RI, RS = 32, 8
CJ, CC = 128, 8
QN, QL = 4, 32
LANES = 128
SHIPS = 32
MIX = 5


def sub_iota():
    return lax.broadcasted_iota(jnp.int32, (8, LANES), 0)


def wide_iota(width):
    return lax.broadcasted_iota(jnp.int32, (8, width), 0)


def from_before(x, k, fill):
    return jnp.where(wide_iota(x.shape[1]) >= k, pltpu.roll(x, k, 0), fill)


def from_after(x, k, fill):
    return jnp.where(wide_iota(x.shape[1]) < 8 - k, pltpu.roll(x, 8 - k, 0), fill)


def prefix_pair(a, b):
    for k in (1, 2, 4):
        b = a * from_before(b, k, 0.0) + b
        a = a * from_before(a, k, 1.0)
    return a, b


def suffix_pair(a, c):
    for k in (1, 2, 4):
        c = c + a * from_after(c, k, 0.0)
        a = a * from_after(a, k, 1.0)
    return a, c


def suffix_bounce(a, d):
    for k in (1, 2, 4):
        d = d + a * from_after(d, k, 0.0) * a
        a = a * from_after(a, k, 1.0)
    return a, d


def carry_factors(a, d):
    count = len(a)
    after_a, after_d = [None] * count, [None] * count
    run_a, run_d = jnp.ones_like(a[0]), jnp.zeros_like(a[0])
    for q in reversed(range(count)):
        after_a[q], after_d[q] = run_a, run_d
        run_d = d[q] + a[q] * run_d * a[q]
        run_a = a[q] * run_a
    before = jnp.ones_like(run_a)
    for k in (1,):
        inclusive, _ = prefix_pair(run_a, jnp.zeros_like(run_a))
        before = from_before(inclusive, k, 1.0)
    all_a, all_d = suffix_bounce(run_a, run_d)
    out_a, out_d = from_after(all_a, 1, 1.0), from_after(all_d, 1, 0.0)
    result = []
    for q in range(count):
        right_a = out_a * after_a[q]
        right_d = after_d[q] + after_a[q] * out_d * after_a[q]
        result.append((before, right_a, before * a[q] * right_d))
        before = before * a[q]
    return result, all_a, all_d


def carry_values(a, b, c, d):
    count = len(a)
    run_a, run_b = a[0], b[0]
    for q in range(1, count):
        run_b = a[q] * run_b + b[q]
        run_a = a[q] * run_a
    _, inclusive = prefix_pair(run_a, run_b)
    left = [from_before(inclusive, 1, 0.0)]
    for q in range(count - 1):
        left.append(a[q] * left[q] + b[q])
    c = [c[q] + d[q] * left[q] for q in range(count)]
    run_c = c[count - 1]
    for q in reversed(range(count - 1)):
        run_c = c[q] + a[q] * run_c
    _, inclusive = suffix_pair(run_a, run_c)
    right = [None] * count
    right[count - 1] = from_after(inclusive, 1, 0.0)
    for q in reversed(range(1, count)):
        right[q - 1] = a[q] * right[q] + c[q]
    return left, right


def total(terms):
    while len(terms) > 1:
        terms = [
            terms[k] + terms[k + 1] if k + 1 < len(terms) else terms[k]
            for k in range(0, len(terms), 2)
        ]
    return terms[0]


def weights(a, d, me, ref):
    count = len(a)
    zero, one = jnp.zeros_like(a[0]), jnp.ones_like(a[0])
    run, from_c = zero, []
    for j in range(count):
        from_c.append(run)
        ref[j, 1] = run
        run = jnp.where(me == j, one, run * a[j])
    left, right = zero, zero
    for j in reversed(range(count)):
        ref[j, 0] = left
        ref[j, 2] = right
        left = jnp.where(me == j, one, left * a[j])
        right = from_c[j] * d[j] + a[j] * right


def kernel(
    nrow,
    ncol,
    depth_h, length_h, srow_h, scol_h, sreach_h, sstr_h,
    pot_h, code_h, surf_h,
    snN, xN, rN, GyC, HyC, inflow,
    cN, pN, sN, prN, uN, GN, HN, bN, fN,
    rT, iaT, pT, uT, GcT, HcT, dT, sT, fT,
    fB, bB, hp, hc,
    eb, lb, ye, yl, xin, xsc, ysc, yad, yfx, xw, yw,
    depth_s, length_s, srow_s, scol_s, sreach_s, sstr_s, s_sem,
    in_sem, h_send, h_recv, e_send, e_recv, l_send, l_recv,
    ye_send, ye_recv, yl_send, yl_recv,
):
    r = lax.axis_index("row")
    c = lax.axis_index("col")

    def loads(src, dst, k):
        return [
            pltpu.make_async_copy(src.at[s], dst.at[:, s, :], in_sem.at[k, s]) for s in range(RS)
        ]

    code_in = loads(code_h, cN, 0)
    pot_in = loads(pot_h, pN, 1)
    surf_in = loads(surf_h, sN, 2)
    small = [
        pltpu.make_async_copy(src, dst, s_sem.at[k])
        for k, (src, dst) in enumerate(
            (
                (depth_h, depth_s), (length_h, length_s), (srow_h, srow_s),
                (scol_h, scol_s), (sreach_h, sreach_s), (sstr_h, sstr_s),
            )
        )
    ]
    for cp in small + code_in + pot_in + surf_in:
        cp.start()

    barrier = pltpu.get_barrier_semaphore()
    north, south = lax.rem(r + nrow - 1, nrow), lax.rem(r + 1, nrow)
    for k in [1, nrow - 1] + list(range(2, nrow - 1)):
        pl.semaphore_signal(
            barrier, inc=1, device_id=(lax.rem(r + k, nrow), c), device_id_type=MESH
        )
    for k in range(1, ncol):
        pl.semaphore_signal(
            barrier, inc=1, device_id=(r, lax.rem(c + k, ncol)), device_id_type=MESH
        )

    for cp in small:
        cp.wait()
    sub = sub_iota()
    tab_len = jnp.zeros((8, LANES), F32)
    tab_dep = jnp.zeros((8, LANES), F32)
    for k in range(8):
        tab_len = jnp.where(sub == k, length_s[k], tab_len)
        tab_dep = jnp.where(sub == k, depth_s[k], tab_dep)
    tab_r = jnp.exp(-1.0 / tab_len)
    tab_w = 1.0 / tab_r
    tab_ia = 1.0 / tab_dep

    def look(tab, idx):
        return jnp.take_along_axis(tab, idx, axis=0)

    params = []
    for k in range(0, SHIPS, 8):
        rows, cols_of, wide, strong = (jnp.zeros((8, LANES), d) for d in (jnp.int32,) * 2 + (F32,) * 2)
        for n in range(8):
            rows = jnp.where(sub == n, srow_s[k + n], rows)
            cols_of = jnp.where(sub == n, scol_s[k + n], cols_of)
            wide = jnp.where(sub == n, (sreach_s[k + n] + 1).astype(F32), wide)
            strong = jnp.where(sub == n, sstr_s[k + n], strong)
        params.append((rows, cols_of, 1.0 / wide, strong))
    lane8 = lax.broadcasted_iota(jnp.int32, (8, LANES), 1)

    def near(at, centre, narrow):
        return jnp.maximum(0.0, 1.0 - jnp.abs(at - centre).astype(F32) * narrow)

    def parts_of(x):
        high = x.astype(jnp.bfloat16).astype(F32)
        rest = x - high
        mid = rest.astype(jnp.bfloat16).astype(F32)
        return high, mid, rest - mid

    pad = jnp.zeros((64, LANES), F32)
    along_y = []
    for g in range(2):
        held = lane8 + g * LANES
        y = r * ROWS + lax.bitwise_and(held, 7) * RI + lax.shift_right_logical(held, 3)
        h, m, l = parts_of(jnp.concatenate([near(y, p[0], p[2]) * p[3] for p in params], axis=0))
        deep = jnp.concatenate([h, h, m, m, h, l, pad], axis=0)
        along_y.append(
            jnp.concatenate([deep[:LANES].T, deep[LANES:].T], axis=1).astype(jnp.bfloat16)
        )
    along_y = jnp.concatenate(along_y, axis=0)
    for cc in range(0, CC, 2):
        wide = []
        for k in range(2):
            x = c * COLS + (cc + k) * LANES + lane8
            h, m, l = parts_of(jnp.concatenate([near(x, p[1], p[2]) for p in params], axis=0))
            wide.append(jnp.concatenate([h, m, h, m, l, h, pad], axis=0).astype(jnp.bfloat16))
        block = jnp.dot(
            along_y, jnp.concatenate(wide, axis=1), preferred_element_type=F32
        )
        prN[:, :, pl.ds(cc * LANES, 2 * LANES)] = block.reshape(RI, RS, 2 * LANES)

    for cp in code_in:
        cp.wait()

    def cols(cc):
        return pl.ds(pl.multiple_of(cc * LANES, LANES), LANES)

    def block_of(ref, g, cc):
        return ref[pl.ds(g * 16, 16), :, cols(cc)].reshape(LANES, LANES)

    def put_t(ref, g, cc, value):
        ref.at[g][pl.ds(cc, CJ, stride=CC), :] = value

    def get_t(ref, g, cc):
        return ref.at[g][pl.ds(cc, CJ, stride=CC), :]

    def blocks(body):
        @pl.loop(0, CC, unroll=8)
        def _(cc):
            for g in range(2):
                body(g, cc)

    def codes_block(g, cc):
        idx = block_of(cN, g, cc).T.reshape(16, 8, LANES)
        for tab, ref in ((tab_r, rT), (tab_ia, iaT)):
            put_t(ref, g, cc, jnp.concatenate([look(tab, idx[k]) for k in range(16)], axis=0))

    blocks(codes_block)

    def row8(j):
        return pl.ds(pl.multiple_of(j * 8, 8), 8)

    one = jnp.ones((8, LANES), F32)
    zero = jnp.zeros((8, LANES), F32)
    chains = [(q, g) for q in range(QN) for g in range(2)]

    def fwd(i, carry):
        new = []
        for n, (q, g) in enumerate(chains):
            at = row8(q * QL + i)
            fT[g, at, :] = carry[n]
            new.append(carry[n] * rT[g, at, :])
        return tuple(new)

    xa = lax.fori_loop(0, QL, fwd, (one,) * 8, unroll=4)

    def bwd(t, carry):
        i = QL - 1 - t
        new = []
        for n, (q, g) in enumerate(chains):
            at = row8(q * QL + i)
            rate = rT[g, at, :]
            grow = carry[2 * n]
            bounce = (1.0 - rate) * fT[g, at, :] + carry[2 * n + 1]
            GcT[g, at, :] = grow
            HcT[g, at, :] = bounce
            new += [rate * grow, rate * bounce]
        return tuple(new)

    ends = lax.fori_loop(0, QL, bwd, (one, zero) * 8, unroll=2)
    xd = ends[1::2]
    xA = [[xa[q * 2 + g] for q in range(QN)] for g in range(2)]
    xD = [[xd[q * 2 + g] for q in range(QN)] for g in range(2)]
    line_a, line_d, x_factors = [], [], []
    for g in range(2):
        factors, all_a, all_d = carry_factors(xA[g], xD[g])
        line_a.append(all_a[0:1])
        line_d.append(all_d[0:1])
        x_factors.append(factors)
        for q in range(QN):
            for k in range(3):
                xsc[g, q, k] = factors[q][k]

    row_peers = sorted(
        ((dx, dy, dc) for dx in range(4) for dy in range(2) for dc in range(2)),
        key=lambda o: -(min(o[0], 4 - o[0]) + 2 * o[1]),
    )
    row_peers = [o for o in row_peers if any(o)]
    col_peers = sorted(
        ((dz, dy) for dz in range(4) for dy in range(2)), key=lambda o: -(min(o[0], 4 - o[0]) + o[1])
    )
    col_peers = [o for o in col_peers if any(o)]

    def to_row(buf, send, recv, k):
        dx, dy, dc = row_peers[k]
        x, y, core = lax.div(c, 4), lax.rem(lax.div(c, 2), 2), lax.rem(c, 2)
        peer = lax.rem(x + dx, 4) * 4 + lax.rem(y + dy, 2) * 2 + lax.rem(core + dc, 2)
        return pltpu.make_async_remote_copy(
            src_ref=buf.at[c],
            dst_ref=buf.at[c],
            send_sem=send,
            recv_sem=recv,
            device_id=(r, peer),
            device_id_type=MESH,
        )

    def to_col(buf, send, recv, k):
        dz, dy = col_peers[k]
        z, y = lax.div(r, 2), lax.rem(r, 2)
        peer = lax.rem(z + dz, 4) * 2 + lax.rem(y + dy, 2)
        return pltpu.make_async_remote_copy(
            src_ref=buf.at[r],
            dst_ref=buf.at[r],
            send_sem=send,
            recv_sem=recv,
            device_id=(peer, c),
            device_id_type=MESH,
        )

    def wait_all(buf, sem, count):
        rest = buf.at[pl.ds(0, count - 1)]
        pltpu.make_async_copy(rest, rest, sem).wait()

    for cp in pot_in:
        cp.wait()
    pl.semaphore_wait(barrier, nrow - 1 + ncol - 1)
    halo = []
    for n, (src_i, src_s, dst_s, target) in enumerate(
        ((RI - 1, RS - 1, 0, south), (0, 0, RS - 1, north))
    ):
        for m, (src, dst) in enumerate(((pN, hp), (cN, hc))):
            halo.append(
                pltpu.make_async_remote_copy(
                    src_ref=src.at[src_i, pl.ds(src_s, 1), :],
                    dst_ref=dst.at[n, pl.ds(dst_s, 1), :],
                    send_sem=h_send.at[n, m],
                    recv_sem=h_recv.at[n, m],
                    device_id=(target, c),
                    device_id_type=MESH,
                )
            )
    for cp in halo:
        cp.start()

    for cp in surf_in:
        cp.wait()

    groups = range(CC)
    col_of = [pl.ds(cc * LANES, LANES) for cc in groups]

    def flux(ia0, ia1, p0, p1):
        return (2.0 / (ia0 + ia1)) * (p1 - p0)

    first, closing = [], []
    for cc in groups:
        at = col_of[cc]
        ia_top, ia_end = look(tab_ia, cN[0, :, at]), look(tab_ia, cN[RI - 1, :, at])
        t = flux(ia_end, pltpu.roll(ia_top, 7, 0), pN[RI - 1, :, at], pltpu.roll(pN[0, :, at], 7, 0))
        closing.append(jnp.where(sub < 7, t, 0.0))
        first += [pltpu.roll(closing[cc], 1, 0), ia_top]

    def flow_row(i, carry):
        new = []
        for cc in groups:
            at = col_of[cc]
            nxt = look(tab_ia, cN[i + 1, :, at])
            t = flux(carry[2 * cc + 1], nxt, pN[i, :, at], pN[i + 1, :, at])
            uN[i, :, at] = sN[i, :, at] + 0.2 * (t - carry[2 * cc])
            new += [t, nxt]
        return tuple(new)

    def turn_back(g, cc):
        rate = get_t(rT, g, cc)
        rate = rate * (1.0 - rate)
        grow = get_t(GcT, g, cc) * rate
        bounce = get_t(HcT, g, cc) * rate
        full, turned = [], []
        for q in range(QN):
            left, right, turn = (xsc[g, q, k, pl.ds(cc, 1), :] for k in range(3))
            rows = slice(q * QL, (q + 1) * QL)
            full.append(grow[rows] * right)
            turned.append(grow[rows] * turn + bounce[rows] * left)
        for value, dst in ((full, GN), (turned, HN)):
            block = jnp.concatenate(value, axis=0).T
            dst[pl.ds(g * 16, 16), :, cols(cc)] = block.reshape(16, 8, LANES)

    def mixed(step, carry):
        g, cc = lax.div(step, CC), lax.rem(step, CC)
        put_t(pT, g, cc, block_of(pN, g, cc).T)
        turn_back(g, cc)
        return flow_row(2 * step + 1, flow_row(2 * step, carry))

    before = lax.fori_loop(0, RI // 2 - 1, mixed, tuple(first), unroll=MIX)
    before = flow_row(RI - 2, before)
    put_t(pT, 1, CC - 1, block_of(pN, 1, CC - 1).T)
    turn_back(1, CC - 1)
    for cc in groups:
        at = col_of[cc]
        uN[RI - 1, :, at] = sN[RI - 1, :, at] + 0.2 * (closing[cc] - before[2 * cc])

    last = CJ * CC - 1
    for g in range(2):
        eb[c, 0, pl.ds(g, 1), :] = line_a[g]
        eb[c, 1, pl.ds(g, 1), :] = line_d[g]
        eb[c, 2, pl.ds(g, 1), :] = pT[g, pl.ds(0, 1), :]
        eb[c, 3, pl.ds(g, 1), :] = pT[g, pl.ds(last, 1), :]
        eb[c, 4, pl.ds(g, 1), :] = iaT[g, pl.ds(0, 1), :]
        eb[c, 5, pl.ds(g, 1), :] = iaT[g, pl.ds(last, 1), :]
        eb[c, 6, pl.ds(g, 1), :] = rT[g, pl.ds(0, 1), :]
        eb[c, 7, pl.ds(g, 1), :] = rT[g, pl.ds(last, 1), :]

    early = [to_row(eb, e_send, e_recv, k) for k in range(ncol - 1)]
    for cp in early:
        cp.start()

    def level_t():
        blocks(lambda g, cc: put_t(uT, g, cc, (block_of(uN, g, cc) + block_of(prN, g, cc)).T))

    level_t()

    flows = []
    for q, g in chains:
        if q == 0:
            t = flux(
                iaT[g, row8(CJ - 1), :], pltpu.roll(iaT[g, row8(0), :], 7, 0),
                pT[g, row8(CJ - 1), :], pltpu.roll(pT[g, row8(0), :], 7, 0),
            )
            flows.append(pltpu.roll(jnp.where(sub < 7, t, 0.0), 1, 0))
        else:
            at, nxt = row8(q * QL - 1), row8(q * QL)
            flows.append(flux(iaT[g, at, :], iaT[g, nxt, :], pT[g, at, :], pT[g, nxt, :]))
    ends_of = [pltpu.roll(flows[g], 7, 0) for g in range(2)]
    ends_of = [jnp.where(sub < 7, t, 0.0) for t in ends_of]

    def source_cell(g, at, t, before, f, sum_c):
        d = t - before
        dT[g, at, :] = d
        value = pT[g, at, :] - 0.2 * (uT[g, at, :] + 0.2 * d)
        rate = rT[g, at, :]
        value = (1.0 - rate) * value
        return value + rate * f, sum_c + value * HcT[g, at, :]

    def source_row(i, carry):
        new = []
        for n, (q, g) in enumerate(chains):
            t0, f, sum_c = carry[3 * n : 3 * n + 3]
            at, nxt = row8(q * QL + i), row8(q * QL + i + 1)
            t = flux(iaT[g, at, :], iaT[g, nxt, :], pT[g, at, :], pT[g, nxt, :])
            new += [t, *source_cell(g, at, t, t0, f, sum_c)]
        return tuple(new)

    init = []
    for n in range(8):
        init += [flows[n], zero, zero]
    sums = lax.fori_loop(0, QL - 1, source_row, tuple(init))
    line_b, line_c = [zero, zero], [zero, zero]
    for n, (q, g) in enumerate(chains):
        t = ends_of[g] if q == QN - 1 else flows[n + 2]
        f, sum_c = source_cell(g, row8((q + 1) * QL - 1), t, *sums[3 * n : 3 * n + 3])
        left, right, turn = x_factors[g][q]
        line_b[g] = line_b[g] + f * right
        line_c[g] = line_c[g] + f * turn + sum_c * left
    line_b = [jnp.sum(x, axis=0, keepdims=True) for x in line_b]
    line_c = [jnp.sum(x, axis=0, keepdims=True) for x in line_c]

    for cp in halo:
        cp.wait_recv()
    lane = lax.broadcasted_iota(jnp.int32, (1, LANES), 1)
    for n, (i, s, has) in enumerate(((0, 0, r > 0), (RI - 1, RS - 1, r < nrow - 1))):
        tot_b, tot_c = zero, zero
        here = jnp.logical_and(sub == s, has)
        for cc in groups:
            at = col_of[cc]
            code = cN[i, :, at]
            other = look(tab_ia, jnp.where(sub == s, hc[n, :, at], 0))
            q = flux(look(tab_ia, code), other, pN[i, :, at], hp[n, :, at])
            q = jnp.where(here, q, 0.0)
            uN[i, :, at] = uN[i, :, at] + 0.2 * q
            q = -0.04 * q * look(tab_w, code)
            tot_b = tot_b + q * GN[i, :, at]
            tot_c = tot_c + q * HN[i, :, at]
        mine = lane == (0 if n == 0 else LANES - 1)
        line_b[n] = line_b[n] + jnp.where(mine, jnp.sum(tot_b), 0.0)
        line_c[n] = line_c[n] + jnp.where(mine, jnp.sum(tot_c), 0.0)
    for g in range(2):
        lb[c, 0, pl.ds(g, 1), :] = line_b[g]
        lb[c, 1, pl.ds(g, 1), :] = line_c[g]
    late = [to_row(lb, l_send, l_recv, k) for k in range(ncol - 1)]
    for cp in late:
        cp.start()

    def rates_row(i, carry):
        new = []
        for cc in groups:
            at = col_of[cc]
            rate = look(tab_r, cN[i, :, at])
            rN[i, :, at] = rate
            fN[i, :, at] = carry[cc]
            new.append(carry[cc] * rate)
        return tuple(new)

    ya = lax.fori_loop(0, RI, rates_row, (one,) * 8, unroll=2)

    def bounce_row(t, carry):
        i = RI - 1 - t
        new = []
        for cc in groups:
            at = col_of[cc]
            rate = rN[i, :, at]
            grow = carry[2 * cc]
            bounce = (1.0 - rate) * fN[i, :, at] + carry[2 * cc + 1]
            GyC[i, :, at] = grow
            HyC[i, :, at] = bounce
            new += [rate * grow, rate * bounce]
        return tuple(new)

    yd = lax.fori_loop(0, RI, bounce_row, (one, zero) * 8, unroll=2)[1::2]
    for cc in groups:
        factors, all_a, all_d = carry_factors([ya[cc]], [yd[cc]])
        for k in range(3):
            ysc[k, cc] = factors[0][k]
        yad[0, cc] = ya[cc]
        yad[1, cc] = yd[cc]
        ye[r, 0, pl.ds(cc, 1), :] = all_a[0:1]
        ye[r, 1, pl.ds(cc, 1), :] = all_d[0:1]
    y_early = [to_col(ye, ye_send, ye_recv, k) for k in range(nrow - 1)]
    for cp in y_early:
        cp.start()

    level_t()

    def x_fwd(i, carry):
        new = []
        for n, (q, g) in enumerate(chains):
            at = row8(q * QL + i)
            rate = rT[g, at, :]
            value = pT[g, at, :] - 0.2 * (uT[g, at, :] + 0.2 * dT[g, at, :])
            f = (1.0 - rate) * value + rate * carry[n]
            fT[g, at, :] = f
            new.append(f)
        return tuple(new)

    xb = lax.fori_loop(0, QL, x_fwd, (zero,) * 8, unroll=2)

    def x_bwd(t, carry):
        i = QL - 1 - t
        new = []
        for n, (q, g) in enumerate(chains):
            at = row8(q * QL + i)
            rate = rT[g, at, :]
            b = (1.0 - rate) * fT[g, at, :] + rate * carry[n]
            sT[g, at, :] = b
            new.append(b)
        return tuple(new)

    xc = lax.fori_loop(0, QL, x_bwd, (zero,) * 8, unroll=2)
    for g in range(2):
        left, right = carry_values(
            xA[g], [xb[q * 2 + g] for q in range(QN)], [xc[q * 2 + g] for q in range(QN)], xD[g]
        )
        for q in range(QN):

            def fix(i, _, g=g, q=q, fl=left[q], br=right[q]):
                at = row8(q * QL + i)
                more = GcT[g, at, :] * br + HcT[g, at, :] * fl
                rate = rT[g, at, :]
                sT[g, at, :] = (1.0 - rate) * (sT[g, at, :] + rate * more)
                return 0

            lax.fori_loop(0, QL, fix, 0, unroll=8)

    def solved_back(g, cc):
        bN[pl.ds(g * 16, 16), :, cols(cc)] = get_t(sT, g, cc).T.reshape(16, 8, LANES)

    blocks(solved_back)

    wait_all(eb, e_recv, ncol)
    nil = jnp.zeros((2, LANES), F32)
    faces = []
    for j in range(ncol - 1):
        faces.append(
            0.04 * flux(eb[j, 5], eb[j + 1, 4], eb[j, 3], eb[j + 1, 2])
        )
    into, gain, back, back_gain = [], [], [], []
    for j in range(ncol):
        r_w, r_e = eb[j, 6], eb[j, 7]
        west = faces[j - 1] if j > 0 else nil
        east = faces[j] if j < ncol - 1 else nil
        out_e = -(1.0 - r_e) * east
        into.append((1.0 - r_w) / r_w * west)
        turn_e = (1.0 - r_e) / r_e * out_e
        gain.append(eb[j, 0] * into[j] + out_e)
        back.append(turn_e)
        back_gain.append(eb[j, 0] * turn_e + eb[j, 1] * into[j])
    weights(
        [eb[j, 0] for j in range(ncol)], [eb[j, 1] for j in range(ncol)], c, xw
    )
    f_in, b_in = nil, nil
    for j in range(ncol):
        f_in = f_in + jnp.where(c == j, into[j], xw[j, 0] * gain[j])
        b_in = b_in + jnp.where(c == j, back[j], 0.0)
        b_in = b_in + xw[j, 1] * back_gain[j] + xw[j, 2] * gain[j]
    wait_all(lb, l_recv, ncol)
    f_in = f_in + total([xw[j, 0] * lb[j, 0] for j in range(ncol)])
    b_in = b_in + total([xw[j, 1] * lb[j, 1] + xw[j, 2] * lb[j, 0] for j in range(ncol)])
    xin[0] = f_in
    xin[1] = b_in
    for g in range(2):
        for src, dst in ((0, fB), (1, bB)):
            line = xin[src, pl.ds(g, 1), :]
            dst[pl.ds(g * 16, 16), :, :] = (
                jnp.broadcast_to(line, (LANES, LANES)).T.reshape(16, 8, LANES)
            )

    def solved_row(i, carry):
        new = []
        fb, bb = fB[i], bB[i]
        for cc in groups:
            at = col_of[cc]
            rate = rN[i, :, at]
            value = bN[i, :, at] + GN[i, :, at] * bb + HN[i, :, at] * fb
            f = value + rate * carry[2 * cc]
            fN[i, :, at] = f
            new += [f, carry[2 * cc + 1] + value * HyC[i, :, at]]
        return tuple(new)

    sums = lax.fori_loop(0, RI, solved_row, (zero,) * 16, unroll=4)
    yb = sums[0::2]
    for cc in groups:
        left, right, turn = (ysc[k, cc] for k in range(3))
        sum_b = yb[cc] * right
        sum_c = yb[cc] * turn + sums[2 * cc + 1] * left
        yl[r, 0, pl.ds(cc, 1), :] = jnp.sum(sum_b, axis=0, keepdims=True)
        yl[r, 1, pl.ds(cc, 1), :] = jnp.sum(sum_c, axis=0, keepdims=True)
    y_late = [to_col(yl, yl_send, yl_recv, k) for k in range(nrow - 1)]
    for cp in y_late:
        cp.start()

    def y_bwd(t, carry):
        i = RI - 1 - t
        new = []
        for cc in groups:
            at = col_of[cc]
            rate = rN[i, :, at]
            b = (1.0 - rate) * fN[i, :, at] + rate * carry[cc]
            xN[i, :, at] = b
            new.append(b)
        return tuple(new)

    yc = lax.fori_loop(0, RI, y_bwd, (zero,) * 8, unroll=2)
    for cc in groups:
        left, right = carry_values([yad[0, cc]], [yb[cc]], [yc[cc]], [yad[1, cc]])
        yfx[0, cc] = left[0]
        yfx[1, cc] = right[0]

    edge_w = jnp.where(c > 0, 1.0, 0.0)
    edge_e = jnp.where(c < ncol - 1, 1.0, 0.0)
    low, high = lax.rem(c + ncol - 1, ncol), lax.rem(c + 1, ncol)
    q_w = flux(eb[c, 4], eb[low, 5], eb[c, 2], eb[low, 3]) * edge_w
    q_e = flux(eb[c, 5], eb[high, 4], eb[c, 3], eb[high, 2]) * edge_e
    for g in range(2):
        dT[g, pl.ds(0, 1), :] = dT[g, pl.ds(0, 1), :] + q_w[g : g + 1]
        dT[g, pl.ds(last, 1), :] = dT[g, pl.ds(last, 1), :] + q_e[g : g + 1]

    def surface_back(g, cc):
        at = (pl.ds(g * 16, 16), slice(None), cols(cc))
        snN[at] = uN[at] + 0.2 * get_t(dT, g, cc).T.reshape(16, 8, LANES)

    blocks(surface_back)

    wait_all(ye, ye_recv, nrow)
    weights([ye[j, 0] for j in range(nrow)], [ye[j, 1] for j in range(nrow)], r, yw)
    for cp in halo:
        cp.wait_send()
    wait_all(eb, e_send, ncol)
    wait_all(lb, l_send, ncol)
    wait_all(ye, ye_send, nrow)
    wait_all(yl, yl_recv, nrow)
    own_f = total([yw[j, 0] * yl[j, 0] for j in range(nrow)])
    own_b = total([yw[j, 1] * yl[j, 1] + yw[j, 2] * yl[j, 0] for j in range(nrow)])
    for cc in groups:
        left, right, turn = (ysc[k, cc] for k in range(3))
        f_row = jnp.broadcast_to(own_f[cc : cc + 1], (8, LANES))
        b_row = jnp.broadcast_to(own_b[cc : cc + 1], (8, LANES))
        inflow[0, cc] = yfx[0, cc] + left * f_row
        inflow[1, cc] = yfx[1, cc] + right * b_row + turn * f_row
    wait_all(yl, yl_send, nrow)


def finish(snN, xN, rN, GyC, HyC, inflow, sn_h, out_h, oN, sem):
    def store(src, dst, k, half):
        rows = pl.ds(half * 16, 16)
        return [
            pltpu.make_async_copy(src.at[rows, s, :], dst.at[s, rows, :], sem.at[k, half, s])
            for s in range(RS)
        ]

    copies = store(snN, sn_h, 0, 0) + store(snN, sn_h, 0, 1)
    for cp in copies:
        cp.start()
    groups = range(CC)
    left = [inflow[0, cc] for cc in groups]
    right = [inflow[1, cc] for cc in groups]

    def last_row(i, _):
        for cc in groups:
            at = pl.ds(cc * LANES, LANES)
            more = GyC[i, :, at] * right[cc] + HyC[i, :, at] * left[cc]
            oN[i, :, at] = xN[i, :, at] + rN[i, :, at] * more
        return 0

    for half in range(2):
        lax.fori_loop(half * 16, half * 16 + 16, last_row, 0, unroll=2)
        new = store(oN, out_h, 1, half)
        for cp in new:
            cp.start()
        copies += new
    for cp in copies:
        cp.wait()


def shards(nrow, ncol, surface, potential, depth_codes, class_depth, class_length, ship_rows,
           ship_cols, ship_reach, ship_strength):
    tile = (RS, RI, COLS)
    natural = pltpu.VMEM((RI, RS, COLS), F32)
    turned = pltpu.VMEM((2, CJ * CC, LANES), F32)
    dma = pltpu.SemaphoreType.DMA
    hbm = pl.BlockSpec(memory_space=pl.ANY)
    vmem = pl.BlockSpec(memory_space=pltpu.VMEM)
    held = pl.pallas_call(
        functools.partial(kernel, nrow, ncol),
        out_shape=[natural] * 5 + [pltpu.VMEM((2, CC, 8, LANES), F32)],
        in_specs=[hbm] * 9,
        out_specs=[vmem] * 6,
        scratch_shapes=[pltpu.VMEM((RI, RS, COLS), jnp.int32)]
        + [natural] * 8
        + [turned] * 9
        + [
            pltpu.VMEM((RI, RS, LANES), F32),
            pltpu.VMEM((RI, RS, LANES), F32),
            pltpu.VMEM((2, 8, COLS), F32),
            pltpu.VMEM((2, 8, COLS), jnp.int32),
            pltpu.VMEM((ncol, 8, 2, LANES), F32),
            pltpu.VMEM((ncol, 2, 2, LANES), F32),
            pltpu.VMEM((nrow, 2, 8, LANES), F32),
            pltpu.VMEM((nrow, 2, 8, LANES), F32),
            pltpu.VMEM((2, 2, LANES), F32),
            pltpu.VMEM((2, QN, 3, 8, LANES), F32),
            pltpu.VMEM((3, CC, 8, LANES), F32),
            pltpu.VMEM((2, CC, 8, LANES), F32),
            pltpu.VMEM((2, CC, 8, LANES), F32),
            pltpu.VMEM((ncol, 3, 2, LANES), F32),
            pltpu.VMEM((nrow, 3, 8, LANES), F32),
            *[pltpu.SMEM((8,), F32)] * 2,
            *[pltpu.SMEM((SHIPS,), jnp.int32)] * 3,
            pltpu.SMEM((SHIPS,), F32),
            dma((6,)),
            dma((3, RS)), dma((2, 2)), dma((2, 2)),
            *[dma] * 8,
        ],
        compiler_params=pltpu.CompilerParams(
            collective_id=0, has_side_effects=True, vmem_limit_bytes=32 * 1024 * 1024
        ),
    )(
        *[
            pltpu.with_memory_space_constraint(x, pltpu.HBM)
            for x in (
                class_depth, class_length, ship_rows, ship_cols, ship_reach, ship_strength,
                potential.reshape(tile), depth_codes.reshape(tile), surface.reshape(tile),
            )
        ]
    )
    surface_next, potential_next = pl.pallas_call(
        finish,
        out_shape=[jax.ShapeDtypeStruct(tile, F32)] * 2,
        in_specs=[vmem] * 6,
        out_specs=[hbm] * 2,
        scratch_shapes=[natural, dma((2, 2, RS))],
        compiler_params=pltpu.CompilerParams(vmem_limit_bytes=16 * 1024 * 1024),
    )(*held)
    return surface_next.reshape(ROWS, COLS), potential_next.reshape(ROWS, COLS)


def solution(mesh):
    in_specs = (P("row", "col"), P("row", "col"), P("row", "col"), P(), P(), P(), P(), P(), P())
    out_specs = (P("row", "col"), P("row", "col"))
    return jax.shard_map(
        functools.partial(shards, mesh.shape["row"], mesh.shape["col"]),
        mesh=mesh, in_specs=in_specs, out_specs=out_specs, check_vma=False,
    )
```
